512 devices in a mesh: row: 16 (over z, core), col: 32 (over y, x).
Axes of the slice: x: 4, y: 8, z: 8, core: 2. Of those that a mesh axis runs over, the one named last changes fastest.
Arguments:
- inverse_block: float32 [8192, 8192], P('row', 'col'), as said below
- panels: bfloat16 [2, 8192, 512], P(None, 'row'), may hold values from -0.09375 to 0.09375
- pattern: int32 [2, 64], replicated, may hold values 0 or 1
Outputs:
- inverse_panel: float32 [2, 8192, 512], P(None, ('row', 'col'))
- update: float32 [2, 512, 512], P(None, 'col')
The draws below stay inside these ranges and needn't reach their ends.
Inputs may be any that keep to these rules, and one draw needn't show every extreme that they name: `pattern`: 1 marks a block of rows in the supernode's structure, 0 a block outside it. `inverse_block`: symmetric.
All inputs are finite; a program needn't handle non-finite values.
Results may differ from the reference program's by a relative error of at most 0.00045.
Values may be sent and summed in bfloat16 or wider, within the bound.
A program may use at most 64 MiB of HBM per device.

```python
import jax
import jax.numpy as jnp
from jax import lax

W = 512
BLOCK = 128
NA = 8192
NB = 64


def draw_inverse_block(key, part):
    key_rough = jax.random.fold_in(key, 11)
    key_diag = jax.random.fold_in(key, 12)
    rough = jax.random.normal(key_rough, (NA, NA), jnp.float32)
    sym = (rough + rough.T) * (0.35 / NA ** 0.5)
    diag_vals = jax.random.uniform(key_diag, (NA,), jnp.float32, 1.0, 2.0)
    return sym + jnp.diag(diag_vals)


def touch_ends(drawn, stream_key, smallest, high):
    spot = [jax.random.randint(jax.random.fold_in(stream_key, axis), (), 0, length) for axis, length in enumerate(drawn.shape)]
    longest = drawn.shape.index(max(drawn.shape))
    next_to = spot[:longest] + [(spot[longest] + 1) % drawn.shape[longest]] + spot[longest + 1:]
    return drawn.at[tuple(spot)].set(smallest).at[tuple(next_to)].set(high)


def level_of(rng, extent, split, least, high):
    gain = 1.0
    for axis_at, blocks in split:
        draws = jax.random.uniform(jax.random.fold_in(jax.random.fold_in(rng, 6), axis_at), (blocks,), jnp.float32, least / len(split), high / len(split))
        gain = gain * jnp.repeat(jnp.exp(draws), extent[axis_at] // blocks).reshape((-1,) + (1,) * (len(extent) - 1 - axis_at))
    return gain


def scatter_about(stream_key, dims, scale, limit, cuts=(), kind=jnp.bfloat16):
    entries = scale * jax.random.normal(stream_key, dims, jnp.float32)
    if cuts:
        entries = entries * level_of(stream_key, dims, cuts, -0.22, 0.18)
    return jnp.clip(entries, -limit, limit).astype(kind)


def setup_inputs(seed: int = 0) -> dict:
    arg_keys = jax.random.split(jax.random.key(seed), 4)
    return {
        "inverse_block": draw_inverse_block(jax.random.fold_in(arg_keys[3], 71), 0),
        "panels": scatter_about(arg_keys[1], (2, NA, W), (NA // 2) ** -0.5, 0.09375, ((1, 16),)),
        "pattern": touch_ends((jax.random.randint(arg_keys[2], (2, NB), 0, 2) < 1).astype(jnp.int32), jax.random.fold_in(arg_keys[2], 1), 0, 1),
    }


def reference(inverse_block, panels, pattern):
    block_ids = jnp.arange(NA, dtype=jnp.int32) // BLOCK
    onehot = block_ids[:, None] == jnp.arange(NB, dtype=jnp.int32)[None, :]
    row_mask = jnp.sum(jnp.where(onehot[None, :, :], pattern[:, None, :], 0), axis=2)
    used = panels * row_mask[:, :, None].astype(jnp.bfloat16)
    used_wide = used.astype(jnp.float32)
    product = jnp.einsum("ij,sjw->siw", inverse_block, used_wide, precision=lax.Precision.HIGHEST)
    inverse_panel = -(product * row_mask[:, :, None].astype(jnp.float32))
    update = -jnp.einsum("siv,siw->svw", used_wide, inverse_panel, precision=lax.Precision.HIGHEST)
    return inverse_panel, update
```

```python
import functools

import jax
import jax.numpy as jnp
from jax import lax
from jax.experimental import pallas as pl
from jax.experimental.pallas import tpu as pltpu
from jax.sharding import PartitionSpec as P

MESH = pl.DeviceIdType.MESH
F32 = jnp.float32
BF16 = jnp.bfloat16
I16 = jnp.int16
NZ, NQ, NX, NY = 8, 2, 4, 8
TOP = 32767.0
TINY = 1e-30


def split(value):
    high = value.astype(BF16)
    return high, (value - high.astype(F32)).astype(BF16)


def kernel(
    pattern, a_hbm, panels_hbm, ip_out, up_out,
    a_v, u_v, lhs, pf, tb, pb, xb, zs, zsc, zr, zrsc, own, ipo, ub, ux, uo, ur, uf,
    in_sem, pf_send, pf_recv, xs_send, xs_recv, zs_send, zr_recv, zc_send, zc_recv,
    ip_send, ip_recv, ux_send, ux_recv, us_send, ur_recv, uf_send, uf_recv,
):
    row = lax.axis_index("row")
    col = lax.axis_index("col")
    z, q = row // 2, row % 2
    y, x = col // 4, col % 4

    def loads():
        yield pltpu.make_async_copy(a_hbm, a_v, in_sem.at[0])
        for p in range(4):
            yield pltpu.make_async_copy(
                panels_hbm.at[p // 2, :, pl.ds((p % 2) * 256, 256)], u_v.at[p], in_sem.at[1 + p]
            )

    for copy in loads():
        copy.start()

    pf_row, pf_col = y * 2 + x % 2, z * 4 + q * 2 + x // 2
    pf_self = jnp.logical_and(pf_row == row, pf_col == col)
    from_row, from_col = y * 2 + x // 2, z * 4 + (x % 2) * 2 + q
    ip_src_col, ip_src_core = row * 2 + col // 16, (col % 16) // 8
    ip_row = y * 2 + x // 2
    ip_col0 = (x % 2) * 16 + q * 8
    ip_has_self = jnp.logical_and(ip_row == row, jnp.logical_and(col >= ip_col0, col < ip_col0 + 8))

    barrier = pltpu.get_barrier_semaphore()

    @pl.loop(1, 16)
    def _(step):
        pl.semaphore_signal(barrier, inc=1, device_id=((row + step) % 16, col), device_id_type=MESH)

    @pl.loop(1, 32)
    def _(step):
        pl.semaphore_signal(barrier, inc=1, device_id=(row, (col + step) % 32), device_id_type=MESH)

    @pl.loop(0, 8)
    def _(step):
        source = step * 2 + ip_src_core

        @pl.when(jnp.logical_or(source != row, ip_src_col != col))
        def _():
            pl.semaphore_signal(barrier, inc=1, device_id=(source, ip_src_col), device_id_type=MESH)

    @pl.when(jnp.logical_not(pf_self))
    def _():
        pl.semaphore_signal(barrier, inc=1, device_id=(from_row, from_col), device_id_type=MESH)

    pl.semaphore_wait(
        barrier, 15 + 31 + 8 + 1 - ip_has_self.astype(jnp.int32) - pf_self.astype(jnp.int32)
    )

    pf_src = panels_hbm.at[y // 4, pl.ds(pl.multiple_of(x * 128, 128), 128), :]
    pf_copy = pltpu.make_async_remote_copy(
        src_ref=pf_src, dst_ref=pf, send_sem=pf_send, recv_sem=pf_recv,
        device_id=(pf_row, pf_col), device_id_type=MESH,
    )

    @pl.when(pf_self)
    def _():
        pltpu.make_async_copy(pf_src, pf, pf_recv).start()

    @pl.when(jnp.logical_not(pf_self))
    def _():
        pf_copy.start()

    copies = list(loads())
    copies[0].wait()
    high, low = split(a_v[...].T)
    lhs[0:256] = high
    lhs[256:512] = low
    for copy in copies[1:]:
        copy.wait()

    def exchange(p):
        return pltpu.make_async_remote_copy(
            src_ref=pb.at[1 - q, pl.ds(2 * p, 2)], dst_ref=xb.at[pl.ds(2 * p, 2)],
            send_sem=xs_send.at[p], recv_sem=xs_recv.at[p],
            device_id=(row + 1 - 2 * q, col), device_id_type=MESH,
        )

    pairs = [(z // 2 + step) % 4 for step in (2, 1, 3, 0)]
    for p in pairs:
        parts = []
        for b in range(4):
            keep = pattern[p // 2, row * 4 + b].astype(F32)
            parts.append(u_v[p, b * 128:(b + 1) * 128] * jnp.full((128, 256), keep, F32).astype(BF16))
        both = jnp.dot(lhs[...], jnp.concatenate(parts, 0), preferred_element_type=F32)
        product = both[0:256] + both[256:512]
        for half in range(2):
            for which in range(2):
                pb[half, 2 * p + which] = product[half * 128:(half + 1) * 128, which * 128:(which + 1) * 128]
        exchange(p).start()

    def to_z(d):
        return (
            pltpu.make_async_remote_copy(
                src_ref=zs.at[d], dst_ref=zr.at[z], send_sem=zs_send.at[d], recv_sem=zr_recv.at[z],
                device_id=(d * 2 + q, col), device_id_type=MESH,
            ),
            pltpu.make_async_remote_copy(
                src_ref=zsc.at[d], dst_ref=zrsc.at[z], send_sem=zc_send.at[d], recv_sem=zc_recv.at[z],
                device_id=(d * 2 + q, col), device_id_type=MESH,
            ),
        )

    for p in pairs:
        exchange(p).wait_recv()
        for which in range(2):
            d = 2 * p + which
            total = pb[q, d] + xb[d]

            @pl.when(d == z)
            def _():
                own[...] = total

            @pl.when(d != z)
            def _():
                top = jnp.maximum(jnp.max(jnp.abs(total), axis=0, keepdims=True), TINY)
                zs[d] = jnp.round(total * (TOP / top)).astype(jnp.int32).astype(I16)
                zsc[d] = jnp.broadcast_to(top * (1.0 / TOP), (8, 128))
                for copy in to_z(d):
                    copy.start()

    pltpu.make_async_copy(pf_src, pf, pf_recv).wait()
    flipped = pf[...].T
    tb[:, 0:128] = flipped
    tb[:, 128:256] = flipped

    for step in (7, 1, 6, 2, 5, 3, 4):
        source = (z + step) % 8
        pltpu.make_async_copy(zr.at[source], zr.at[source], zr_recv.at[source]).wait()
        pltpu.make_async_copy(zrsc.at[source], zrsc.at[source], zc_recv.at[source]).wait()
        own[...] += zr[source].astype(jnp.int32).astype(F32) * zrsc[source][0:1]
    mask = pattern[z // 4, 2 * col + q].astype(F32)
    block = own[...] * (-mask)
    ipo[...] = block

    ip_dst = ip_out.at[z // 4, :, pl.ds(pl.multiple_of((z % 4) * 128, 128), 128)]

    def to_owner(kk):
        return pltpu.make_async_remote_copy(
            src_ref=ipo.at[pl.ds(kk * 16, 16)], dst_ref=ip_dst, send_sem=ip_send.at[kk], recv_sem=ip_recv,
            device_id=(ip_row, ip_col0 + kk), device_id_type=MESH,
        )

    @pl.loop(0, 8)
    def _(kk):
        is_self = jnp.logical_and(ip_row == row, ip_col0 + kk == col)

        @pl.when(is_self)
        def _():
            pltpu.make_async_copy(ipo.at[pl.ds(kk * 16, 16)], ip_dst, ip_recv).start()

        @pl.when(jnp.logical_not(is_self))
        def _():
            to_owner(kk).start()

    high, low = split(block * mask)
    part = -jnp.dot(tb[...], jnp.concatenate([high, low], 0), preferred_element_type=F32)
    part = part.reshape(32, 2, 8, 128)
    for half in range(2):
        ub[half] = part[:, half]
    to_sibling = pltpu.make_async_remote_copy(
        src_ref=ub.at[1 - q], dst_ref=ux, send_sem=ux_send, recv_sem=ux_recv,
        device_id=(row + 1 - 2 * q, col), device_id_type=MESH,
    )
    to_sibling.start()
    to_sibling.wait_recv()
    uo[...] = ub[q] + ux[...]

    def to_col(step):
        there = (col + step) % 32
        return pltpu.make_async_remote_copy(
            src_ref=uo.at[there], dst_ref=ur.at[col], send_sem=us_send, recv_sem=ur_recv,
            device_id=(row, there), device_id_type=MESH,
        )

    @pl.loop(1, 32)
    def _(step):
        to_col(step).start()

    ur[col] = uo[col]
    arrived = ur.at[pl.ds(0, 31)]
    pltpu.make_async_copy(arrived, arrived, ur_recv).wait()
    uf[...] = jnp.sum(ur[...], axis=0)

    up_dst = up_out.at[
        z // 4, pl.ds(pl.multiple_of(q * 8, 8), 8), pl.ds(pl.multiple_of((z % 4) * 128, 128), 128)
    ]
    pltpu.make_async_copy(uf, up_dst, uf_recv).start()

    def to_row(step):
        return pltpu.make_async_remote_copy(
            src_ref=uf, dst_ref=up_dst, send_sem=uf_send.at[step], recv_sem=uf_recv,
            device_id=((row + step) % 16, col), device_id_type=MESH,
        )

    @pl.loop(1, 16)
    def _(step):
        to_row(step).start()

    @pl.when(jnp.logical_not(pf_self))
    def _():
        pf_copy.wait_send()

    for p in range(4):
        exchange(p).wait_send()

    @pl.loop(1, 8)
    def _(step):
        for copy in to_z((z + step) % 8):
            copy.wait_send()

    @pl.loop(0, 8)
    def _(kk):
        @pl.when(jnp.logical_or(ip_row != row, ip_col0 + kk != col))
        def _():
            to_owner(kk).wait_send()

    to_sibling.wait_send()
    pltpu.make_async_copy(arrived, arrived, us_send).wait()

    @pl.loop(1, 16)
    def _(step):
        to_row(step).wait_send()

    pltpu.make_async_copy(ip_out, ip_out, ip_recv).wait()
    pltpu.make_async_copy(up_out, up_out, uf_recv).wait()


def shards(inverse_block, panels, pattern):
    dma = pltpu.SemaphoreType.DMA
    return pl.pallas_call(
        kernel,
        out_shape=(
            jax.ShapeDtypeStruct((2, 16, 512), F32),
            jax.ShapeDtypeStruct((2, 16, 512), F32),
        ),
        in_specs=[
            pl.BlockSpec(memory_space=pltpu.SMEM),
            pl.BlockSpec(memory_space=pl.ANY),
            pl.BlockSpec(memory_space=pl.ANY),
        ],
        out_specs=(pl.BlockSpec(memory_space=pl.ANY), pl.BlockSpec(memory_space=pl.ANY)),
        scratch_shapes=[
            pltpu.VMEM((512, 256), F32),
            pltpu.VMEM((4, 512, 256), BF16),
            pltpu.VMEM((512, 512), BF16),
            pltpu.VMEM((128, 512), BF16),
            pltpu.VMEM((512, 256), BF16),
            pltpu.VMEM((2, 8, 128, 128), F32),
            pltpu.VMEM((8, 128, 128), F32),
            pltpu.VMEM((8, 128, 128), I16),
            pltpu.VMEM((8, 8, 128), F32),
            pltpu.VMEM((8, 128, 128), I16),
            pltpu.VMEM((8, 8, 128), F32),
            pltpu.VMEM((128, 128), F32),
            pltpu.VMEM((128, 128), F32),
            pltpu.VMEM((2, 32, 8, 128), F32),
            pltpu.VMEM((32, 8, 128), F32),
            pltpu.VMEM((32, 8, 128), F32),
            pltpu.VMEM((32, 8, 128), F32),
            pltpu.VMEM((8, 128), F32),
            dma((5,)), dma, dma, dma((4,)), dma((4,)), dma((8,)), dma((8,)), dma((8,)), dma((8,)),
            dma((8,)), dma, dma, dma, dma, dma, dma((16,)), dma,
        ],
        compiler_params=pltpu.CompilerParams(
            collective_id=0, has_side_effects=True, vmem_limit_bytes=32 * 1024 * 1024
        ),
        cost_estimate=pl.CostEstimate(flops=2 ** 29, bytes_accessed=2 ** 21, transcendentals=0),
    )(pattern, inverse_block, panels)


def solution(mesh):
    return jax.shard_map(
        shards,
        mesh=mesh,
        in_specs=(P("row", "col"), P(None, "row", None), P()),
        out_specs=(P(None, ("row", "col"), None), P(None, "col", None)),
        check_vma=False,
    )
```

```python
import functools

import jax
import jax.numpy as jnp
from jax import lax
from jax.experimental import pallas as pl
from jax.experimental.pallas import tpu as pltpu
from jax.sharding import PartitionSpec as P

MESH = pl.DeviceIdType.MESH
F32 = jnp.float32
BF16 = jnp.bfloat16
I16 = jnp.int16
NZ, NQ, NX, NY = 8, 2, 4, 8
TOP = 32767.0
TINY = 1e-30


def split(value):
    high = value.astype(BF16)
    return high, (value - high.astype(F32)).astype(BF16)


def kernel(
    pattern, a_hbm, panels_hbm, ip_out, up_out,
    a_v, u_v, lhs, pm, pf, tb, pb, xb, zs, zsc, zr, zrsc, own, ipo, im, ub, ux, uo, ur, uf,
    in_sem, pm_send, pm_recv, pf_send, pf_recv, xs_send, xs_recv, zs_send, zr_recv, zc_send, zc_recv,
    im_send, im_recv, ip_send, ip_recv, ux_send, ux_recv, us_send, ur_recv, uf_send, uf_recv,
):
    row = lax.axis_index("row")
    col = lax.axis_index("col")
    z, q = row // 2, row % 2
    y, x = col // 4, col % 4
    sibling = (row + 1 - 2 * q, col)

    def remote(src, dst, send, recv, there):
        return pltpu.make_async_remote_copy(
            src_ref=src, dst_ref=dst, send_sem=send, recv_sem=recv, device_id=there, device_id_type=MESH
        )

    def arrival(ref, sem):
        return pltpu.make_async_copy(ref, ref, sem)

    def start(here, src, dst, send, recv, there):
        @pl.when(here)
        def _():
            pltpu.make_async_copy(src, dst, recv).start()

        @pl.when(jnp.logical_not(here))
        def _():
            remote(src, dst, send, recv, there).start()

    def sent(here, src, dst, send, recv, there):
        @pl.when(jnp.logical_not(here))
        def _():
            remote(src, dst, send, recv, there).wait_send()

    def far_first(step, count):
        half = (step + 1) // 2
        return count // 2 + jnp.where(step % 2 == 0, half, -half)

    pairs = [(z // 2 + step) % 4 for step in (2, 1, 3, 0)]

    def load_u(p):
        return pltpu.make_async_copy(
            panels_hbm.at[p // 2, :, pl.ds(pl.multiple_of((p % 2) * 256, 256), 256)], u_v.at[p], in_sem.at[1 + p]
        )

    load_a = pltpu.make_async_copy(a_hbm, a_v, in_sem.at[0])
    load_a.start()
    for p in pairs:
        load_u(p).start()

    barrier = pltpu.get_barrier_semaphore()

    @pl.loop(0, 31)
    def _(step):
        there = (row, (col + far_first(step, 32)) % 32)
        pl.semaphore_signal(barrier, inc=1, device_id=there, device_id_type=MESH)

    @pl.loop(0, 15)
    def _(step):
        there = ((row + far_first(step, 16)) % 16, col)
        pl.semaphore_signal(barrier, inc=1, device_id=there, device_id_type=MESH)

    load_a.wait()
    high, low = split(a_v[...].T)
    lhs[0:256] = high
    lhs[256:512] = low
    for p in pairs:
        load_u(p).wait()
        parts = []
        for b in range(4):
            keep = pattern[p // 2, row * 4 + b].astype(F32)
            parts.append(u_v[p, b * 128:(b + 1) * 128] * jnp.full((128, 256), keep, F32).astype(BF16))
        both = jnp.dot(lhs[...], jnp.concatenate(parts, 0), preferred_element_type=F32)
        product = both[0:256] + both[256:512]
        for half in range(2):
            for which in range(2):
                pb[half, 2 * p + which] = product[half * 128:(half + 1) * 128, which * 128:(which + 1) * 128]

    pl.semaphore_wait(barrier, 46)

    pm_z, pm_q = (16 - y - z) % 8, x % 2
    pm_args = (
        jnp.logical_and(pm_z == z, pm_q == q),
        panels_hbm.at[pm_z // 4, pl.ds(pl.multiple_of(x * 128, 128), 128), :], pm.at[q],
        pm_send, pm_recv.at[q], (pm_z * 2 + pm_q, col),
    )
    start(*pm_args)

    def exchange(p):
        return remote(
            pb.at[1 - q, pl.ds(2 * p, 2)], xb.at[pl.ds(2 * p, 2)], xs_send.at[p], xs_recv.at[p], sibling
        )

    for p in pairs:
        exchange(p).start()

    def to_z(d):
        there = (d * 2 + q, col)
        return (
            remote(zs.at[d], zr.at[z], zs_send.at[d], zr_recv.at[z], there),
            remote(zsc.at[d], zrsc.at[z], zc_send.at[d], zc_recv.at[z], there),
        )

    for p in pairs:
        exchange(p).wait_recv()
        for which in range(2):
            d = 2 * p + which
            total = pb[q, d] + xb[d]

            @pl.when(d == z)
            def _():
                own[...] = total

            @pl.when(d != z)
            def _():
                top = jnp.maximum(jnp.max(jnp.abs(total), axis=0, keepdims=True), TINY)
                zs[d] = jnp.round(total * (TOP / top)).astype(jnp.int32).astype(I16)
                zsc[d] = jnp.broadcast_to(top * (1.0 / TOP), (8, 128))
                for copy in to_z(d):
                    copy.start()

    def pf_args(core):
        there_x, there_y = core * 2 + x // 2, pm_z
        return (
            jnp.logical_and(there_x == x, there_y == y),
            pm.at[core], pf, pf_send.at[core], pf_recv, (row, there_y * 4 + there_x),
        )

    forwards_pf = x % 2 == q

    @pl.when(forwards_pf)
    def _():
        for core in range(2):
            arrival(pm.at[core], pm_recv.at[core]).wait()
            start(*pf_args(core))

    arrival(pf, pf_recv).wait()
    flipped = pf[...].T
    tb[:, 0:128] = flipped
    tb[:, 128:256] = flipped

    for step in (7, 1, 6, 2, 5, 3, 4):
        source = (z + step) % 8
        arrival(zr.at[source], zr_recv.at[source]).wait()
        arrival(zrsc.at[source], zc_recv.at[source]).wait()
        own[...] += zr[source].astype(jnp.int32).astype(F32) * zrsc[source][0:1]
    mask = pattern[z // 4, 2 * col + q].astype(F32)
    block = own[...] * (-mask)
    ipo[...] = block

    def im_args(kk):
        there_x, there_y = kk % 4, (x % 2) * 4 + q * 2 + kk // 4
        return (
            jnp.logical_and(there_x == x, there_y == y),
            ipo.at[pl.ds(pl.multiple_of(kk * 16, 16), 16)], im.at[y * 2 + x // 2], im_send.at[kk], im_recv,
            (row, there_y * 4 + there_x),
        )

    @pl.loop(0, 8)
    def _(kk):
        start(*im_args(kk))

    high, low = split(block * mask)
    part = -jnp.dot(tb[...], jnp.concatenate([high, low], 0), preferred_element_type=F32)
    part = part.reshape(32, 2, 8, 128)
    for half in range(2):
        ub[half] = part[:, half]
    to_sibling = remote(ub.at[1 - q], ux, ux_send, ux_recv, sibling)
    to_sibling.start()
    to_sibling.wait_recv()
    uo[...] = ub[q] + ux[...]

    def to_col(step):
        there = (col + far_first(step, 32)) % 32
        return remote(uo.at[there], ur.at[col], us_send, ur_recv, (row, there))

    @pl.loop(0, 31)
    def _(step):
        to_col(step).start()

    ur[col] = uo[col]

    def ip_args(there):
        return (
            there == row,
            im.at[there], ip_out.at[z // 4, :, pl.ds(pl.multiple_of((z % 4) * 128, 128), 128)],
            ip_send.at[there], ip_recv, (there, col),
        )

    forwards_ip = (y % 4) // 2 == q

    @pl.when(forwards_ip)
    def _():
        arrival(im, im_recv).wait()

        @pl.loop(0, 16)
        def _(step):
            start(*ip_args((row + 8 + step) % 16))

    arrived = ur.at[pl.ds(0, 31)]
    arrival(arrived, ur_recv).wait()
    uf[...] = jnp.sum(ur[...], axis=0)

    up_dst = up_out.at[
        z // 4, pl.ds(pl.multiple_of(q * 8, 8), 8), pl.ds(pl.multiple_of((z % 4) * 128, 128), 128)
    ]

    def to_row(step):
        return remote(uf, up_dst, uf_send.at[step], uf_recv, ((row + far_first(step, 16)) % 16, col))

    @pl.loop(0, 15)
    def _(step):
        to_row(step).start()

    pltpu.make_async_copy(uf, up_dst, uf_recv).start()

    sent(*pm_args)

    @pl.when(forwards_pf)
    def _():
        for core in range(2):
            sent(*pf_args(core))

    for p in range(4):
        exchange(p).wait_send()

    @pl.loop(1, 8)
    def _(step):
        for copy in to_z((z + step) % 8):
            copy.wait_send()

    @pl.loop(0, 8)
    def _(kk):
        sent(*im_args(kk))

    to_sibling.wait_send()
    arrival(arrived, us_send).wait()

    @pl.when(forwards_ip)
    def _():
        @pl.loop(0, 16)
        def _(there):
            sent(*ip_args(there))

    @pl.loop(0, 15)
    def _(step):
        to_row(step).wait_send()

    arrival(ip_out, ip_recv).wait()
    arrival(up_out, uf_recv).wait()


def shards(inverse_block, panels, pattern):
    dma = pltpu.SemaphoreType.DMA
    return pl.pallas_call(
        kernel,
        out_shape=(
            jax.ShapeDtypeStruct((2, 16, 512), F32),
            jax.ShapeDtypeStruct((2, 16, 512), F32),
        ),
        in_specs=[
            pl.BlockSpec(memory_space=pltpu.SMEM),
            pl.BlockSpec(memory_space=pl.ANY),
            pl.BlockSpec(memory_space=pl.ANY),
        ],
        out_specs=(pl.BlockSpec(memory_space=pl.ANY), pl.BlockSpec(memory_space=pl.ANY)),
        scratch_shapes=[
            pltpu.VMEM((512, 256), F32),
            pltpu.VMEM((4, 512, 256), BF16),
            pltpu.VMEM((512, 512), BF16),
            pltpu.VMEM((2, 128, 512), BF16),
            pltpu.VMEM((128, 512), BF16),
            pltpu.VMEM((512, 256), BF16),
            pltpu.VMEM((2, 8, 128, 128), F32),
            pltpu.VMEM((8, 128, 128), F32),
            pltpu.VMEM((8, 128, 128), I16),
            pltpu.VMEM((8, 8, 128), F32),
            pltpu.VMEM((8, 128, 128), I16),
            pltpu.VMEM((8, 8, 128), F32),
            pltpu.VMEM((128, 128), F32),
            pltpu.VMEM((128, 128), F32),
            pltpu.VMEM((16, 16, 128), F32),
            pltpu.VMEM((2, 32, 8, 128), F32),
            pltpu.VMEM((32, 8, 128), F32),
            pltpu.VMEM((32, 8, 128), F32),
            pltpu.VMEM((32, 8, 128), F32),
            pltpu.VMEM((8, 128), F32),
            dma((5,)), dma, dma((2,)), dma((2,)), dma, dma((4,)), dma((4,)), dma((8,)), dma((8,)), dma((8,)), dma((8,)),
            dma((8,)), dma, dma((16,)), dma, dma, dma, dma, dma, dma((16,)), dma,
        ],
        compiler_params=pltpu.CompilerParams(
            collective_id=0, has_side_effects=True, vmem_limit_bytes=60 * 1024 * 1024
        ),
        cost_estimate=pl.CostEstimate(flops=2 ** 29, bytes_accessed=2 ** 21, transcendentals=0),
    )(pattern, inverse_block, panels)


def solution(mesh):
    return jax.shard_map(
        shards,
        mesh=mesh,
        in_specs=(P("row", "col"), P(None, "row", None), P()),
        out_specs=(P(None, ("row", "col"), None), P(None, "col", None)),
        check_vma=False,
    )
```

```python
import functools

import jax
import jax.numpy as jnp
from jax import lax
from jax.experimental import pallas as pl
from jax.experimental.pallas import tpu as pltpu
from jax.sharding import PartitionSpec as P

MESH = pl.DeviceIdType.MESH
F32 = jnp.float32
BF16 = jnp.bfloat16
I16 = jnp.int16
NZ, NQ, NX, NY = 8, 2, 4, 8
TOP = 32767.0
TINY = 1e-30


def split(value):
    high = value.astype(BF16)
    return high, (value - high.astype(F32)).astype(BF16)


def kernel(
    pattern, a_hbm, panels_hbm, ip_out, up_out,
    a_v, u_v, lhs, pm, pf, tb, pb, xb, zs, zsc, zr, zrsc, own, im, ub, ux, uo, ur, uf, ipo, up_all,
    in_sem, pm_send, pm_recv, pf_send, pf_recv, xs_send, xs_recv, zs_send, zr_recv, zc_send, zc_recv,
    im_send, im_recv, ip_send, ip_recv, ux_send, ux_recv, us_send, ur_recv, uf_send, uf_recv,
):
    row = lax.axis_index("row")
    col = lax.axis_index("col")
    z, q = row // 2, row % 2
    y, x = col // 4, col % 4
    sibling = (row + 1 - 2 * q, col)

    def remote(src, dst, send, recv, there):
        return pltpu.make_async_remote_copy(
            src_ref=src, dst_ref=dst, send_sem=send, recv_sem=recv, device_id=there, device_id_type=MESH
        )

    def arrival(ref, sem):
        return pltpu.make_async_copy(ref, ref, sem)

    def start(here, src, dst, send, recv, there):
        @pl.when(here)
        def _():
            pltpu.make_async_copy(src, dst, recv).start()

        @pl.when(jnp.logical_not(here))
        def _():
            remote(src, dst, send, recv, there).start()

    def sent(here, src, dst, send, recv, there):
        @pl.when(jnp.logical_not(here))
        def _():
            remote(src, dst, send, recv, there).wait_send()

    def far_first(step, count):
        half = (step + 1) // 2
        return count // 2 + jnp.where(step % 2 == 0, half, -half)

    def pair(step):
        return (z // 2 + jnp.where(step == 0, 2, jnp.where(step == 3, 0, 2 * step - 1))) % 4

    def load_u(p):
        return pltpu.make_async_copy(
            panels_hbm.at[p // 2, :, pl.ds(pl.multiple_of((p % 2) * 256, 256), 256)], u_v.at[p], in_sem.at[1 + p]
        )

    load_a = pltpu.make_async_copy(a_hbm, a_v, in_sem.at[0])
    load_a.start()
    for step in range(4):
        load_u(pair(step)).start()

    barrier = pltpu.get_barrier_semaphore()

    @pl.loop(0, 31)
    def _(step):
        there = (row, (col + far_first(step, 32)) % 32)
        pl.semaphore_signal(barrier, inc=1, device_id=there, device_id_type=MESH)

    @pl.loop(0, 15)
    def _(step):
        there = ((row + far_first(step, 16)) % 16, col)
        pl.semaphore_signal(barrier, inc=1, device_id=there, device_id_type=MESH)

    load_a.wait()
    high, low = split(a_v[...].T)
    lhs[0:256] = high
    lhs[256:512] = low

    @pl.loop(0, 4)
    def _(step):
        p = pair(step)
        load_u(p).wait()
        parts = []
        for b in range(4):
            keep = pattern[p // 2, row * 4 + b].astype(F32)
            parts.append(u_v[p, b * 128:(b + 1) * 128] * jnp.full((128, 256), keep, F32).astype(BF16))
        both = jnp.dot(lhs[...], jnp.concatenate(parts, 0), preferred_element_type=F32)
        product = both[0:256] + both[256:512]
        for half in range(2):
            for which in range(2):
                first = which * 128 + half * 64
                pb[half, 2 * p + which] = product[first:first + 64]

    pl.semaphore_wait(barrier, 46)

    pm_z = (2 * z + 12 - y) % 8
    pm_slot = ((y + 9 - z) % 8) // 4
    sends_pm = q == x // 2
    hands_on = (y + z) % 2 == 0

    def pm_args(core):
        first = (x % 2) * 256 + (pm_z % 2) * 128 + core * 64
        return (
            jnp.logical_and(pm_z == z, q == core),
            panels_hbm.at[pm_z // 4, pl.ds(pl.multiple_of(first, 64), 64), :], pm.at[pm_slot],
            pm_send.at[core], pm_recv.at[pm_slot], (pm_z * 2 + core, col),
        )

    def pf_args(turn):
        via = ((y + z) // 2 + 2 + 4 * turn) % 8
        slot = ((y + 9 - via) % 8) // 4
        return slot, (via == y, pm.at[slot], pf, pf_send.at[slot], pf_recv, (row, via * 4 + x))

    @pl.when(sends_pm)
    def _():
        for core in range(2):
            start(*pm_args(core))

    def exchange(p):
        return remote(
            pb.at[1 - q, pl.ds(2 * p, 2)], xb.at[pl.ds(2 * p, 2)], xs_send.at[p], xs_recv.at[p], sibling
        )

    for step in range(4):
        exchange(pair(step)).start()

    def to_z(d):
        there = (d * 2 + q, col)
        return (
            remote(zs.at[d], zr.at[z], zs_send.at[d], zr_recv.at[z], there),
            remote(zsc.at[d], zrsc.at[z], zc_send.at[d], zc_recv.at[z], there),
        )

    @pl.loop(0, 8)
    def _(step):
        p, which = pair(step // 2), step % 2
        d = 2 * p + which

        @pl.when(which == 0)
        def _():
            exchange(p).wait_recv()

        total = pb[q, d] + xb[d]

        @pl.when(d == z)
        def _():
            own[...] = total

        @pl.when(d != z)
        def _():
            top = jnp.maximum(jnp.max(jnp.abs(total), axis=0, keepdims=True), TINY)
            zs[d] = jnp.round(total * (TOP / top)).astype(jnp.int32).astype(I16)
            zsc[d] = top * (1.0 / TOP)
            for copy in to_z(d):
                copy.start()

    @pl.when(hands_on)
    def _():
        for turn in range(2):
            slot, args = pf_args(turn)
            arrival(pm.at[slot], pm_recv.at[slot]).wait()
            start(*args)

    arrival(pf, pf_recv).wait()
    flipped = pf[...].T
    tb[:, 0:64] = flipped
    tb[:, 64:128] = flipped

    @pl.loop(0, 7)
    def _(step):
        source = (z + far_first(6 - step, 8)) % 8
        arrival(zr.at[source], zr_recv.at[source]).wait()
        arrival(zrsc.at[source], zc_recv.at[source]).wait()
        own[...] += zr[source].astype(jnp.int32).astype(F32) * zrsc[source]
    mask = pattern[z // 4, 2 * col + z % 2].astype(F32)
    block = own[...] * (-mask)
    ipo[...] = block

    def im_args(kk):
        there_x, there_y = kk, (x % 2) * 4 + (z % 2) * 2 + q
        return (
            jnp.logical_and(there_x == x, there_y == y),
            ipo.at[pl.ds(pl.multiple_of(kk * 16, 16), 16)], im.at[y * 2 + x // 2], im_send.at[kk], im_recv,
            (row, there_y * 4 + there_x),
        )

    @pl.loop(0, 4)
    def _(kk):
        start(*im_args(kk))

    high, low = split(block * mask)
    part = -jnp.dot(tb[...], jnp.concatenate([high, low], 0), preferred_element_type=F32)
    for half in range(2):
        ub[half] = part[:, half * 128:(half + 1) * 128].reshape(32, 16, 128)
    to_sibling = remote(ub.at[1 - q], ux, ux_send, ux_recv, sibling)
    to_sibling.start()
    to_sibling.wait_recv()
    uo[...] = ub[q] + ux[...]

    def to_col(step):
        there = (col + far_first(step, 32)) % 32
        return remote(uo.at[there], ur.at[col], us_send, ur_recv, (row, there))

    @pl.loop(0, 31)
    def _(step):
        to_col(step).start()

    ur[col] = uo[col]

    def ip_args(there):
        return (
            there == row,
            im.at[there], ip_out.at[z // 4, :, pl.ds(pl.multiple_of((z // 2 % 2) * 256, 256), 256)],
            ip_send.at[there], ip_recv, (there, col),
        )

    forwards_ip = jnp.logical_and((y % 4) // 2 == z % 2, y % 2 == q)

    @pl.when(forwards_ip)
    def _():
        arrival(im, im_recv).wait()

        @pl.loop(0, 16)
        def _(step):
            start(*ip_args((row + 8 + step) % 16))

    arrived = ur.at[pl.ds(0, 31)]
    arrival(arrived, ur_recv).wait()
    uf[...] = jnp.sum(ur[...], axis=0)

    up_dst = up_all.at[row]

    def to_row(step):
        return remote(uf, up_dst, uf_send.at[step], uf_recv, ((row + far_first(step, 16)) % 16, col))

    @pl.loop(0, 15)
    def _(step):
        to_row(step).start()

    pltpu.make_async_copy(uf, up_dst, uf_recv).start()

    @pl.when(sends_pm)
    def _():
        for core in range(2):
            sent(*pm_args(core))

    @pl.when(hands_on)
    def _():
        for turn in range(2):
            sent(*pf_args(turn)[1])

    for p in range(4):
        exchange(p).wait_send()

    @pl.loop(1, 8)
    def _(step):
        for copy in to_z((z + step) % 8):
            copy.wait_send()

    @pl.loop(0, 4)
    def _(kk):
        sent(*im_args(kk))

    to_sibling.wait_send()
    arrival(arrived, us_send).wait()

    @pl.when(forwards_ip)
    def _():
        @pl.loop(0, 16)
        def _(there):
            sent(*ip_args(there))

    @pl.loop(0, 15)
    def _(step):
        to_row(step).wait_send()

    arrival(up_all, uf_recv).wait()
    for k in range(8):
        first = 4 * (k // 2) + k % 2
        up_out[k // 4, :, (k % 4) * 128:(k % 4 + 1) * 128] = up_all[first] + up_all[first + 2]
    arrival(ip_out, ip_recv).wait()


def shards(inverse_block, panels, pattern):
    dma = pltpu.SemaphoreType.DMA
    return pl.pallas_call(
        kernel,
        out_shape=(
            jax.ShapeDtypeStruct((2, 16, 512), F32),
            jax.ShapeDtypeStruct((2, 16, 512), F32),
        ),
        in_specs=[
            pl.BlockSpec(memory_space=pltpu.SMEM),
            pl.BlockSpec(memory_space=pl.ANY),
            pl.BlockSpec(memory_space=pl.ANY),
        ],
        out_specs=(pl.BlockSpec(memory_space=pl.ANY), pl.BlockSpec(memory_space=pltpu.VMEM)),
        scratch_shapes=[
            pltpu.VMEM((512, 256), F32),
            pltpu.VMEM((4, 512, 256), BF16),
            pltpu.VMEM((512, 512), BF16),
            pltpu.VMEM((2, 64, 512), BF16),
            pltpu.VMEM((64, 512), BF16),
            pltpu.VMEM((512, 128), BF16),
            pltpu.VMEM((2, 8, 64, 256), F32),
            pltpu.VMEM((8, 64, 256), F32),
            pltpu.VMEM((8, 64, 256), I16),
            pltpu.VMEM((8, 1, 256), F32),
            pltpu.VMEM((8, 64, 256), I16),
            pltpu.VMEM((8, 1, 256), F32),
            pltpu.VMEM((64, 256), F32),
            pltpu.VMEM((16, 16, 256), F32),
            pltpu.VMEM((2, 32, 16, 128), F32),
            pltpu.VMEM((32, 16, 128), F32),
            pltpu.VMEM((32, 16, 128), F32),
            pltpu.VMEM((32, 16, 128), F32),
            pltpu.VMEM((16, 128), F32),
            pltpu.VMEM((64, 256), F32),
            pltpu.VMEM((16, 16, 128), F32),
            dma((5,)), dma((2,)), dma((2,)), dma((2,)), dma, dma((4,)), dma((4,)), dma((8,)), dma((8,)), dma((8,)),
            dma((8,)), dma((4,)), dma, dma((16,)), dma, dma, dma, dma, dma, dma((16,)), dma,
        ],
        compiler_params=pltpu.CompilerParams(
            collective_id=0, has_side_effects=True, vmem_limit_bytes=60 * 1024 * 1024
        ),
        cost_estimate=pl.CostEstimate(flops=2 ** 29, bytes_accessed=2 ** 21, transcendentals=0),
    )(pattern, inverse_block, panels)


def solution(mesh):
    return jax.shard_map(
        shards,
        mesh=mesh,
        in_specs=(P("row", "col"), P(None, "row", None), P()),
        out_specs=(P(None, ("row", "col"), None), P(None, "col", None)),
        check_vma=False,
    )
```

```python
import functools

import jax
import jax.numpy as jnp
from jax import lax
from jax.experimental import pallas as pl
from jax.experimental.pallas import tpu as pltpu
from jax.sharding import PartitionSpec as P

MESH = pl.DeviceIdType.MESH
F32 = jnp.float32
BF16 = jnp.bfloat16
I16 = jnp.int16
NZ, NQ, NX, NY = 8, 2, 4, 8
TOP = 32767.0
TINY = 1e-30


def split(value):
    high = value.astype(BF16)
    return high, (value - high.astype(F32)).astype(BF16)


def kernel(
    pattern_hbm, a_hbm, panels_hbm, ip_out, up_out,
    pattern, a_v, u_v, lhs, pm, pf, tb, pb, xb, zs, zsc, zr, zrsc, own, im, ub, ux, uq, usc, ur, ursc, uf, ipo, up_all, fin,
    in_sem, pm_send, pm_recv, pf_send, pf_recv, xs_send, xs_recv, zs_send, zr_recv, zc_send, zc_recv,
    im_send, im_recv, ip_send, ip_recv, ux_send, ux_recv, us_send, ur_recv, uc_send, uc_recv, uf_send, uf_recv, fin_send, fin_recv,
):
    row = lax.axis_index("row")
    col = lax.axis_index("col")
    z, q = row // 2, row % 2
    y, x = col // 4, col % 4
    sibling = (row + 1 - 2 * q, col)

    def remote(src, dst, send, recv, there):
        return pltpu.make_async_remote_copy(
            src_ref=src, dst_ref=dst, send_sem=send, recv_sem=recv, device_id=there, device_id_type=MESH
        )

    def arrival(ref, sem):
        return pltpu.make_async_copy(ref, ref, sem)

    def start(here, src, dst, send, recv, there):
        @pl.when(here)
        def _():
            pltpu.make_async_copy(src, dst, recv).start()

        @pl.when(jnp.logical_not(here))
        def _():
            remote(src, dst, send, recv, there).start()

    def sent(here, src, dst, send, recv, there):
        @pl.when(jnp.logical_not(here))
        def _():
            remote(src, dst, send, recv, there).wait_send()

    def far_first(step, count):
        half = (step + 1) // 2
        return count // 2 + jnp.where(step % 2 == 0, half, -half)

    def pair(step):
        return (z // 2 + jnp.where(step == 0, 2, jnp.where(step == 3, 0, 2 * step - 1))) % 4

    def load_u(p):
        return pltpu.make_async_copy(
            panels_hbm.at[p // 2, :, pl.ds(pl.multiple_of((p % 2) * 256, 256), 256)], u_v.at[p], in_sem.at[1 + p]
        )

    load_pattern = pltpu.make_async_copy(pattern_hbm, pattern, in_sem.at[5])
    load_a = pltpu.make_async_copy(a_hbm, a_v, in_sem.at[0])
    load_a.start()
    load_pattern.start()
    for step in range(4):
        load_u(pair(step)).start()

    barrier = pltpu.get_barrier_semaphore()

    @pl.loop(0, 31)
    def _(step):
        there = (row, (col + far_first(step, 32)) % 32)
        pl.semaphore_signal(barrier, inc=1, device_id=there, device_id_type=MESH)

    @pl.loop(0, 15)
    def _(step):
        there = ((row + far_first(step, 16)) % 16, col)
        pl.semaphore_signal(barrier, inc=1, device_id=there, device_id_type=MESH)

    load_a.wait()
    high, low = split(a_v[...].T)
    lhs[0:256] = high
    lhs[256:512] = low
    load_pattern.wait()

    @pl.loop(0, 4)
    def _(step):
        p = pair(step)
        load_u(p).wait()
        parts = []
        for b in range(4):
            keep = pattern[p // 2, row * 4 + b].astype(F32)
            parts.append(u_v[p, b * 128:(b + 1) * 128] * jnp.full((128, 256), keep, F32).astype(BF16))
        both = jnp.dot(lhs[...], jnp.concatenate(parts, 0), preferred_element_type=F32)
        product = both[0:256] + both[256:512]
        for half in range(2):
            for which in range(2):
                first = which * 128 + half * 64
                pb[half, 2 * p + which] = product[first:first + 64]

    pl.semaphore_wait(barrier, 46)

    pm_z = (2 * z + 12 - y) % 8
    pm_slot = ((y + 9 - z) % 8) // 4
    sends_pm = q == x // 2
    hands_on = (y + z) % 2 == 0

    def pm_args(core):
        first = (x % 2) * 256 + (pm_z % 2) * 128 + core * 64
        return (
            jnp.logical_and(pm_z == z, q == core),
            panels_hbm.at[pm_z // 4, pl.ds(pl.multiple_of(first, 64), 64), :], pm.at[pm_slot],
            pm_send.at[core], pm_recv.at[pm_slot], (pm_z * 2 + core, col),
        )

    def pf_args(turn):
        via = ((y + z) // 2 + 2 + 4 * turn) % 8
        slot = ((y + 9 - via) % 8) // 4
        return slot, (via == y, pm.at[slot], pf, pf_send.at[slot], pf_recv, (row, via * 4 + x))

    @pl.when(sends_pm)
    def _():
        for core in range(2):
            start(*pm_args(core))

    def exchange(p):
        return remote(
            pb.at[1 - q, pl.ds(2 * p, 2)], xb.at[pl.ds(2 * p, 2)], xs_send.at[p], xs_recv.at[p], sibling
        )

    for step in range(4):
        exchange(pair(step)).start()

    def to_z(d):
        there = (d * 2 + q, col)
        return (
            remote(zs.at[d], zr.at[z], zs_send.at[d], zr_recv.at[z], there),
            remote(zsc.at[d], zrsc.at[z], zc_send.at[d], zc_recv.at[z], there),
        )

    @pl.loop(0, 8)
    def _(step):
        p, which = pair(step // 2), step % 2
        d = 2 * p + which

        @pl.when(which == 0)
        def _():
            exchange(p).wait_recv()

        total = pb[q, d] + xb[d]

        @pl.when(d == z)
        def _():
            own[...] = total

        @pl.when(d != z)
        def _():
            top = jnp.maximum(jnp.max(jnp.abs(total), axis=0, keepdims=True), TINY)
            zs[d] = jnp.round(total * (TOP / top)).astype(jnp.int32).astype(I16)
            zsc[d] = top * (1.0 / TOP)
            for copy in to_z(d):
                copy.start()

    @pl.when(hands_on)
    def _():
        for turn in range(2):
            slot, args = pf_args(turn)
            arrival(pm.at[slot], pm_recv.at[slot]).wait()
            start(*args)

    arrival(pf, pf_recv).wait()
    flipped = pf[...].T
    tb[:, 0:64] = flipped
    tb[:, 64:128] = flipped

    @pl.loop(0, 7)
    def _(step):
        source = (z + far_first(6 - step, 8)) % 8
        arrival(zr.at[source], zr_recv.at[source]).wait()
        arrival(zrsc.at[source], zc_recv.at[source]).wait()
        own[...] += zr[source].astype(jnp.int32).astype(F32) * zrsc[source]
    mask = pattern[z // 4, 2 * col + z % 2].astype(F32)
    block = own[...] * (-mask)
    ipo[...] = block

    def im_args(kk):
        there_x, there_y = kk, (x % 2) * 4 + (z % 2) * 2 + q
        return (
            jnp.logical_and(there_x == x, there_y == y),
            ipo.at[pl.ds(pl.multiple_of(kk * 16, 16), 16)], im.at[y * 2 + x // 2], im_send.at[kk], im_recv,
            (row, there_y * 4 + there_x),
        )

    high, low = split(block * mask)
    part = -jnp.dot(tb[...], jnp.concatenate([high, low], 0), preferred_element_type=F32)
    part = part.reshape(16, 2, 16, 256)
    for half in range(2):
        ub[half] = part[:, half]
    to_sibling = remote(ub.at[1 - q], ux, ux_send, ux_recv, sibling)
    to_sibling.start()
    to_sibling.wait_recv()

    def to_col(t):
        there = (row, 2 * t + q)
        return (
            remote(uq.at[t], ur.at[col], us_send.at[t], ur_recv, there),
            remote(usc.at[t], ursc.at[col], uc_send.at[t], uc_recv, there),
        )

    sums_here = col % 2 == q

    @pl.loop(0, 16)
    def _(step):
        t = (col // 2 + far_first(step, 16)) % 16
        total = ub[q, t] + ux[t]
        top = jnp.maximum(jnp.max(jnp.abs(total), axis=0, keepdims=True), TINY)
        uq[t] = jnp.round(total * (TOP / top)).astype(jnp.int32).astype(I16)
        usc[t] = top * (1.0 / TOP)

        @pl.when(2 * t + q != col)
        def _():
            for copy in to_col(t):
                copy.start()

    @pl.loop(0, 4)
    def _(kk):
        start(*im_args(kk))

    def ip_args(there):
        return (
            there == row,
            im.at[there], ip_out.at[z // 4, :, pl.ds(pl.multiple_of((z // 2 % 2) * 256, 256), 256)],
            ip_send.at[there], ip_recv, (there, col),
        )

    forwards_ip = jnp.logical_and((y % 4) // 2 == z % 2, y % 2 == q)

    def to_row(step):
        there = ((z + far_first(step, 8)) % 8 * 2 + q, col)
        return remote(uf, up_all.at[z], uf_send.at[step], uf_recv, there)

    finish = remote(fin, up_out, fin_send, fin_recv, sibling)

    @pl.when(sums_here)
    def _():
        ur[col] = uq[col // 2]
        ursc[col] = usc[col // 2]
        arrival(ur.at[pl.ds(0, 31)], ur_recv).wait()
        arrival(ursc.at[pl.ds(0, 31)], uc_recv).wait()
        uf[...] = jnp.zeros_like(uf)

        @pl.loop(0, 32)
        def _(k):
            uf[...] += ur[k].astype(jnp.int32).astype(F32) * ursc[k]

        @pl.loop(0, 7)
        def _(step):
            to_row(step).start()
        up_all[z] = uf[...]

    @pl.when(forwards_ip)
    def _():
        arrival(im, im_recv).wait()

        @pl.loop(0, 16)
        def _(step):
            start(*ip_args((row + 8 + step) % 16))

    @pl.when(sums_here)
    def _():
        arrival(up_all.at[pl.ds(0, 7)], uf_recv).wait()
        for k in range(4):
            fin[k // 2, :, (k % 2) * 256:(k % 2 + 1) * 256] = up_all[2 * k] + up_all[2 * k + 1]
        finish.start()
        pltpu.make_async_copy(fin, up_out, fin_recv).start()

    @pl.when(sends_pm)
    def _():
        for core in range(2):
            sent(*pm_args(core))

    @pl.when(hands_on)
    def _():
        for turn in range(2):
            sent(*pf_args(turn)[1])

    for p in range(4):
        exchange(p).wait_send()

    @pl.loop(1, 8)
    def _(step):
        for copy in to_z((z + step) % 8):
            copy.wait_send()

    @pl.loop(0, 4)
    def _(kk):
        sent(*im_args(kk))

    to_sibling.wait_send()

    @pl.loop(0, 16)
    def _(t):
        @pl.when(2 * t + q != col)
        def _():
            for copy in to_col(t):
                copy.wait_send()

    @pl.when(forwards_ip)
    def _():
        @pl.loop(0, 16)
        def _(there):
            sent(*ip_args(there))

    @pl.when(sums_here)
    def _():
        @pl.loop(0, 7)
        def _(step):
            to_row(step).wait_send()

        finish.wait_send()

    arrival(ip_out, ip_recv).wait()
    arrival(up_out, fin_recv).wait()


def shards(inverse_block, panels, pattern):
    dma = pltpu.SemaphoreType.DMA
    return pl.pallas_call(
        kernel,
        out_shape=(
            jax.ShapeDtypeStruct((2, 16, 512), F32),
            jax.ShapeDtypeStruct((2, 16, 512), F32),
        ),
        in_specs=[
            pl.BlockSpec(memory_space=pl.ANY),
            pl.BlockSpec(memory_space=pl.ANY),
            pl.BlockSpec(memory_space=pl.ANY),
        ],
        out_specs=(pl.BlockSpec(memory_space=pl.ANY), pl.BlockSpec(memory_space=pl.ANY)),
        scratch_shapes=[
            pltpu.SMEM((2, 64), jnp.int32),
            pltpu.VMEM((512, 256), F32),
            pltpu.VMEM((4, 512, 256), BF16),
            pltpu.VMEM((512, 512), BF16),
            pltpu.VMEM((2, 64, 512), BF16),
            pltpu.VMEM((64, 512), BF16),
            pltpu.VMEM((512, 128), BF16),
            pltpu.VMEM((2, 8, 64, 256), F32),
            pltpu.VMEM((8, 64, 256), F32),
            pltpu.VMEM((8, 64, 256), I16),
            pltpu.VMEM((8, 1, 256), F32),
            pltpu.VMEM((8, 64, 256), I16),
            pltpu.VMEM((8, 1, 256), F32),
            pltpu.VMEM((64, 256), F32),
            pltpu.VMEM((16, 16, 256), F32),
            pltpu.VMEM((2, 16, 16, 256), F32),
            pltpu.VMEM((16, 16, 256), F32),
            pltpu.VMEM((16, 16, 256), I16),
            pltpu.VMEM((16, 1, 256), F32),
            pltpu.VMEM((32, 16, 256), I16),
            pltpu.VMEM((32, 1, 256), F32),
            pltpu.VMEM((16, 256), F32),
            pltpu.VMEM((64, 256), F32),
            pltpu.VMEM((8, 16, 256), F32),
            pltpu.VMEM((2, 16, 512), F32),
            dma((6,)), dma((2,)), dma((2,)), dma((2,)), dma, dma((4,)), dma((4,)), dma((8,)), dma((8,)), dma((8,)),
            dma((8,)), dma((4,)), dma, dma((16,)), dma, dma, dma, dma((16,)), dma, dma((16,)), dma, dma((7,)), dma, dma, dma,
        ],
        compiler_params=pltpu.CompilerParams(
            collective_id=0, has_side_effects=True, vmem_limit_bytes=56250000
        ),
        cost_estimate=pl.CostEstimate(flops=2 ** 29, bytes_accessed=2 ** 21, transcendentals=0),
    )(pattern, inverse_block, panels)


def solution(mesh):
    return jax.shard_map(
        shards,
        mesh=mesh,
        in_specs=(P("row", "col"), P(None, "row", None), P()),
        out_specs=(P(None, ("row", "col"), None), P(None, "col", None)),
        check_vma=False,
    )
```

```python
import functools

import jax
import jax.numpy as jnp
from jax import lax
from jax.experimental import pallas as pl
from jax.experimental.pallas import tpu as pltpu
from jax.sharding import PartitionSpec as P

MESH = pl.DeviceIdType.MESH
F32 = jnp.float32
BF16 = jnp.bfloat16
I16 = jnp.int16
NZ, NQ, NX, NY = 8, 2, 4, 8
TOP = 32767.0
TINY = 1e-30


def split(value):
    high = value.astype(BF16)
    return high, (value - high.astype(F32)).astype(BF16)


def kernel(
    pattern_hbm, a_hbm, panels_hbm, ip_out, up_out,
    pattern, a_v, u_v, lhs, pm, pf, tb, pb, xb, zs, zsc, zr, zrsc, own, im, ub, ux, uq, usc, ur, ursc, uf, ipo, up_all, fin,
    in_sem, pm_send, pm_recv, pf_send, pf_recv, xs_send, xs_recv, zs_send, zr_recv, zc_send, zc_recv,
    im_send, im_recv, ip_send, ip_recv, ux_send, ux_recv, us_send, ur_recv, uc_send, uc_recv, uf_send, uf_recv, fin_send, fin_recv, ready,
):
    row = lax.axis_index("row")
    col = lax.axis_index("col")
    z, q = row // 2, row % 2
    y, x = col // 4, col % 4
    sibling = (row + 1 - 2 * q, col)

    def remote(src, dst, send, recv, there):
        return pltpu.make_async_remote_copy(
            src_ref=src, dst_ref=dst, send_sem=send, recv_sem=recv, device_id=there, device_id_type=MESH
        )

    def arrival(ref, sem):
        return pltpu.make_async_copy(ref, ref, sem)

    def start(here, src, dst, send, recv, there):
        @pl.when(here)
        def _():
            pltpu.make_async_copy(src, dst, recv).start()

        @pl.when(jnp.logical_not(here))
        def _():
            remote(src, dst, send, recv, there).start()

    def sent(here, src, dst, send, recv, there):
        @pl.when(jnp.logical_not(here))
        def _():
            remote(src, dst, send, recv, there).wait_send()

    def far_first(step, count):
        half = (step + 1) // 2
        return count // 2 + jnp.where(step % 2 == 0, half, -half)

    def pair(step):
        return (z // 2 + jnp.where(step == 0, 2, jnp.where(step == 3, 0, 2 * step - 1))) % 4

    def load_u(p):
        return pltpu.make_async_copy(
            panels_hbm.at[p // 2, :, pl.ds(pl.multiple_of((p % 2) * 256, 256), 256)], u_v.at[p], in_sem.at[1 + p]
        )

    load_pattern = pltpu.make_async_copy(pattern_hbm, pattern, in_sem.at[5])
    load_a = pltpu.make_async_copy(a_hbm, a_v, in_sem.at[0])
    load_a.start()
    load_pattern.start()
    for step in range(4):
        load_u(pair(step)).start()

    barrier = pltpu.get_barrier_semaphore()

    @pl.loop(0, 7)
    def _(step):
        there = ((z + far_first(step, 8)) % 8 * 2, col)
        pl.semaphore_signal(barrier, inc=1, device_id=there, device_id_type=MESH)

    @pl.when(q == 1)
    def _():
        pl.semaphore_signal(barrier, inc=1, device_id=sibling, device_id_type=MESH)

    @pl.loop(0, 31)
    def _(step):
        there = (z * 2 + 1, (col + far_first(step, 32)) % 32)
        pl.semaphore_signal(barrier, inc=1, device_id=there, device_id_type=MESH)

    def hear(core, count):
        @pl.when(q == core)
        def _():
            pl.semaphore_wait(barrier, count)
            pl.semaphore_signal(ready, inc=1, device_id=sibling, device_id_type=MESH)

        @pl.when(q != core)
        def _():
            pl.semaphore_wait(ready, 1)

    hear(0, 15)

    pm_z = (2 * z + 12 - y) % 8
    pm_slot = ((y + 9 - z) % 8) // 4
    sends_pm = q == x // 2
    hands_on = (y + z) % 2 == 0

    def pm_args(core):
        first = (x % 2) * 256 + (pm_z % 2) * 128 + core * 64
        return (
            jnp.logical_and(pm_z == z, q == core),
            panels_hbm.at[pm_z // 4, pl.ds(pl.multiple_of(first, 64), 64), :], pm.at[pm_slot],
            pm_send.at[core], pm_recv.at[pm_slot], (pm_z * 2 + core, col),
        )

    def pf_args(turn):
        via = ((y + z) // 2 + 2 + 4 * turn) % 8
        slot = ((y + 9 - via) % 8) // 4
        return slot, (via == y, pm.at[slot], pf, pf_send.at[slot], pf_recv, (row, via * 4 + x))

    @pl.when(sends_pm)
    def _():
        for core in range(2):
            start(*pm_args(core))

    load_a.wait()
    high, low = split(a_v[...].T)
    lhs[0:256] = high
    lhs[256:512] = low
    load_pattern.wait()

    @pl.loop(0, 4)
    def _(step):
        p = pair(step)
        load_u(p).wait()
        parts = []
        for b in range(4):
            keep = pattern[p // 2, row * 4 + b].astype(F32)
            parts.append(u_v[p, b * 128:(b + 1) * 128] * jnp.full((128, 256), keep, F32).astype(BF16))
        both = jnp.dot(lhs[...], jnp.concatenate(parts, 0), preferred_element_type=F32)
        product = both[0:256] + both[256:512]
        for half in range(2):
            for which in range(2):
                first = which * 128 + half * 64
                pb[half, 2 * p + which] = product[first:first + 64]

    def exchange(p):
        return remote(
            pb.at[1 - q, pl.ds(2 * p, 2)], xb.at[pl.ds(2 * p, 2)], xs_send.at[p], xs_recv.at[p], sibling
        )

    for step in range(4):
        exchange(pair(step)).start()

    def to_z(d):
        there = (d * 2 + q, col)
        return (
            remote(zs.at[d], zr.at[z], zs_send.at[d], zr_recv.at[z], there),
            remote(zsc.at[d], zrsc.at[z], zc_send.at[d], zc_recv.at[z], there),
        )

    hear(1, 62)

    @pl.when(hands_on)
    def _():
        for turn in range(2):
            slot, args = pf_args(turn)
            arrival(pm.at[slot], pm_recv.at[slot]).wait()
            start(*args)

    @pl.loop(0, 8)
    def _(step):
        p, which = pair(step // 2), step % 2
        d = 2 * p + which

        @pl.when(which == 0)
        def _():
            exchange(p).wait_recv()

        total = pb[q, d] + xb[d]

        @pl.when(d == z)
        def _():
            own[...] = total

        @pl.when(d != z)
        def _():
            top = jnp.maximum(jnp.max(jnp.abs(total), axis=0, keepdims=True), TINY)
            zs[d] = jnp.round(total * (TOP / top)).astype(jnp.int32).astype(I16)
            zsc[d] = top * (1.0 / TOP)
            for copy in to_z(d):
                copy.start()

    arrival(pf, pf_recv).wait()
    flipped = pf[...].T
    tb[:, 0:64] = flipped
    tb[:, 64:128] = flipped

    @pl.loop(0, 7)
    def _(step):
        source = (z + far_first(6 - step, 8)) % 8
        arrival(zr.at[source], zr_recv.at[source]).wait()
        arrival(zrsc.at[source], zc_recv.at[source]).wait()
        own[...] += zr[source].astype(jnp.int32).astype(F32) * zrsc[source]
    mask = pattern[z // 4, 2 * col + z % 2].astype(F32)
    block = own[...] * (-mask)
    ipo[...] = block

    def im_args(kk):
        there_x, there_y = kk, (x % 2) * 4 + (z % 2) * 2 + q
        return (
            jnp.logical_and(there_x == x, there_y == y),
            ipo.at[pl.ds(pl.multiple_of(kk * 16, 16), 16)], im.at[y * 2 + x // 2], im_send.at[kk], im_recv,
            (row, there_y * 4 + there_x),
        )

    high, low = split(block * mask)
    part = -jnp.dot(tb[...], jnp.concatenate([high, low], 0), preferred_element_type=F32)
    part = part.reshape(16, 2, 16, 256)
    for half in range(2):
        ub[half] = part[:, half]
    to_sibling = remote(ub.at[1 - q], ux, ux_send, ux_recv, sibling)
    to_sibling.start()
    to_sibling.wait_recv()

    def to_col(t):
        there = (row, 2 * t + q)
        return (
            remote(uq.at[t], ur.at[col], us_send.at[t], ur_recv, there),
            remote(usc.at[t], ursc.at[col], uc_send.at[t], uc_recv, there),
        )

    sums_here = col % 2 == q

    @pl.loop(0, 16)
    def _(step):
        t = (col // 2 + far_first(step, 16)) % 16
        total = ub[q, t] + ux[t]
        top = jnp.maximum(jnp.max(jnp.abs(total), axis=0, keepdims=True), TINY)
        uq[t] = jnp.round(total * (TOP / top)).astype(jnp.int32).astype(I16)
        usc[t] = top * (1.0 / TOP)

        @pl.when(2 * t + q != col)
        def _():
            for copy in to_col(t):
                copy.start()

    @pl.loop(0, 4)
    def _(kk):
        start(*im_args(kk))

    def ip_args(there):
        return (
            there == row,
            im.at[there], ip_out.at[z // 4, :, pl.ds(pl.multiple_of((z // 2 % 2) * 256, 256), 256)],
            ip_send.at[there], ip_recv, (there, col),
        )

    forwards_ip = jnp.logical_and((y % 4) // 2 == z % 2, y % 2 == q)

    def to_row(step):
        there = ((z + far_first(step, 8)) % 8 * 2 + q, col)
        return remote(uf, up_all.at[z], uf_send.at[step], uf_recv, there)

    finish = remote(fin, up_out, fin_send, fin_recv, sibling)

    @pl.when(sums_here)
    def _():
        ur[col] = uq[col // 2]
        ursc[col] = usc[col // 2]
        arrival(ur.at[pl.ds(0, 31)], ur_recv).wait()
        arrival(ursc.at[pl.ds(0, 31)], uc_recv).wait()
        uf[...] = jnp.zeros_like(uf)

        @pl.loop(0, 32)
        def _(k):
            uf[...] += ur[k].astype(jnp.int32).astype(F32) * ursc[k]

        @pl.loop(0, 7)
        def _(step):
            to_row(step).start()
        up_all[z] = uf[...]

    @pl.when(forwards_ip)
    def _():
        arrival(im, im_recv).wait()

        @pl.loop(0, 16)
        def _(step):
            start(*ip_args((row + 8 + step) % 16))

    @pl.when(sums_here)
    def _():
        arrival(up_all.at[pl.ds(0, 7)], uf_recv).wait()
        for k in range(4):
            fin[k // 2, :, (k % 2) * 256:(k % 2 + 1) * 256] = up_all[2 * k] + up_all[2 * k + 1]
        finish.start()
        pltpu.make_async_copy(fin, up_out, fin_recv).start()

    @pl.when(sends_pm)
    def _():
        for core in range(2):
            sent(*pm_args(core))

    @pl.when(hands_on)
    def _():
        for turn in range(2):
            sent(*pf_args(turn)[1])

    for p in range(4):
        exchange(p).wait_send()

    @pl.loop(1, 8)
    def _(step):
        for copy in to_z((z + step) % 8):
            copy.wait_send()

    @pl.loop(0, 4)
    def _(kk):
        sent(*im_args(kk))

    to_sibling.wait_send()

    @pl.loop(0, 16)
    def _(t):
        @pl.when(2 * t + q != col)
        def _():
            for copy in to_col(t):
                copy.wait_send()

    @pl.when(forwards_ip)
    def _():
        @pl.loop(0, 16)
        def _(there):
            sent(*ip_args(there))

    @pl.when(sums_here)
    def _():
        @pl.loop(0, 7)
        def _(step):
            to_row(step).wait_send()

        finish.wait_send()

    arrival(ip_out, ip_recv).wait()
    arrival(up_out, fin_recv).wait()


def shards(inverse_block, panels, pattern):
    dma = pltpu.SemaphoreType.DMA
    return pl.pallas_call(
        kernel,
        out_shape=(
            jax.ShapeDtypeStruct((2, 16, 512), F32),
            jax.ShapeDtypeStruct((2, 16, 512), F32),
        ),
        in_specs=[
            pl.BlockSpec(memory_space=pl.ANY),
            pl.BlockSpec(memory_space=pl.ANY),
            pl.BlockSpec(memory_space=pl.ANY),
        ],
        out_specs=(pl.BlockSpec(memory_space=pl.ANY), pl.BlockSpec(memory_space=pl.ANY)),
        scratch_shapes=[
            pltpu.SMEM((2, 64), jnp.int32),
            pltpu.VMEM((512, 256), F32),
            pltpu.VMEM((4, 512, 256), BF16),
            pltpu.VMEM((512, 512), BF16),
            pltpu.VMEM((2, 64, 512), BF16),
            pltpu.VMEM((64, 512), BF16),
            pltpu.VMEM((512, 128), BF16),
            pltpu.VMEM((2, 8, 64, 256), F32),
            pltpu.VMEM((8, 64, 256), F32),
            pltpu.VMEM((8, 64, 256), I16),
            pltpu.VMEM((8, 1, 256), F32),
            pltpu.VMEM((8, 64, 256), I16),
            pltpu.VMEM((8, 1, 256), F32),
            pltpu.VMEM((64, 256), F32),
            pltpu.VMEM((16, 16, 256), F32),
            pltpu.VMEM((2, 16, 16, 256), F32),
            pltpu.VMEM((16, 16, 256), F32),
            pltpu.VMEM((16, 16, 256), I16),
            pltpu.VMEM((16, 1, 256), F32),
            pltpu.VMEM((32, 16, 256), I16),
            pltpu.VMEM((32, 1, 256), F32),
            pltpu.VMEM((16, 256), F32),
            pltpu.VMEM((64, 256), F32),
            pltpu.VMEM((8, 16, 256), F32),
            pltpu.VMEM((2, 16, 512), F32),
            dma((6,)), dma((2,)), dma((2,)), dma((2,)), dma, dma((4,)), dma((4,)), dma((8,)), dma((8,)), dma((8,)),
            dma((8,)), dma((4,)), dma, dma((16,)), dma, dma, dma, dma((16,)), dma, dma((16,)), dma, dma((7,)), dma, dma, dma,
            pltpu.SemaphoreType.REGULAR,
        ],
        compiler_params=pltpu.CompilerParams(
            collective_id=0, has_side_effects=True, vmem_limit_bytes=56250000
        ),
        cost_estimate=pl.CostEstimate(flops=2 ** 29, bytes_accessed=2 ** 21, transcendentals=0),
    )(pattern, inverse_block, panels)


def solution(mesh):
    return jax.shard_map(
        shards,
        mesh=mesh,
        in_specs=(P("row", "col"), P(None, "row", None), P()),
        out_specs=(P(None, ("row", "col"), None), P(None, "col", None)),
        check_vma=False,
    )
```

```python
import functools

import jax
import jax.numpy as jnp
from jax import lax
from jax.experimental import pallas as pl
from jax.experimental.pallas import tpu as pltpu
from jax.sharding import PartitionSpec as P

MESH = pl.DeviceIdType.MESH
F32 = jnp.float32
BF16 = jnp.bfloat16
I16 = jnp.int16
NZ, NQ, NX, NY = 8, 2, 4, 8
TOP = 32767.0
TINY = 1e-30


def split(value):
    high = value.astype(BF16)
    return high, (value - high.astype(F32)).astype(BF16)


def kernel(
    pattern_hbm, a_hbm, panels_hbm, ip_out, up_out,
    pattern, a_v, u_v, lhs, pm, pf, tb, pb, xb, zs, zsc, zr, zrsc, own, im, ub_rhs, ub, ux, uq, usc, ur, ursc, uf, ipo, up_all, fin,
    in_sem, pm_send, pm_recv, pf_send, pf_recv, xs_send, xs_recv, zs_send, zr_recv, zc_send, zc_recv,
    im_send, im_recv, ip_send, ip_recv, ux_send, ux_recv, us_send, ur_recv, uc_send, uc_recv, uf_send, uf_recv, fin_send, fin_recv, ready,
):
    row = lax.axis_index("row")
    col = lax.axis_index("col")
    z, q = row // 2, row % 2
    y, x = col // 4, col % 4
    sibling = (row + 1 - 2 * q, col)

    def remote(src, dst, send, recv, there):
        return pltpu.make_async_remote_copy(
            src_ref=src, dst_ref=dst, send_sem=send, recv_sem=recv, device_id=there, device_id_type=MESH
        )

    def arrival(ref, sem):
        return pltpu.make_async_copy(ref, ref, sem)

    def start(here, src, dst, send, recv, there):
        @pl.when(here)
        def _():
            pltpu.make_async_copy(src, dst, recv).start()

        @pl.when(jnp.logical_not(here))
        def _():
            remote(src, dst, send, recv, there).start()

    def sent(here, src, dst, send, recv, there):
        @pl.when(jnp.logical_not(here))
        def _():
            remote(src, dst, send, recv, there).wait_send()

    def far_first(step, count):
        half = (step + 1) // 2
        return count // 2 + jnp.where(step % 2 == 0, half, -half)

    def pair(step):
        return (z // 2 + jnp.where(step == 0, 2, jnp.where(step == 3, 0, 2 * step - 1))) % 4

    def load_u(p):
        return pltpu.make_async_copy(
            panels_hbm.at[p // 2, :, pl.ds(pl.multiple_of((p % 2) * 256, 256), 256)], u_v.at[p], in_sem.at[1 + p]
        )

    load_pattern = pltpu.make_async_copy(pattern_hbm, pattern, in_sem.at[5])
    load_a = pltpu.make_async_copy(a_hbm, a_v, in_sem.at[0])
    load_a.start()
    load_pattern.start()
    for step in range(4):
        load_u(pair(step)).start()

    barrier = pltpu.get_barrier_semaphore()

    @pl.loop(0, 7)
    def _(step):
        there = ((z + far_first(step, 8)) % 8 * 2, col)
        pl.semaphore_signal(barrier, inc=1, device_id=there, device_id_type=MESH)

    @pl.when(q == 1)
    def _():
        pl.semaphore_signal(barrier, inc=1, device_id=sibling, device_id_type=MESH)

    @pl.loop(0, 31)
    def _(step):
        there = (z * 2 + 1, (col + far_first(step, 32)) % 32)
        pl.semaphore_signal(barrier, inc=1, device_id=there, device_id_type=MESH)

    def hear(core, count):
        @pl.when(q == core)
        def _():
            pl.semaphore_wait(barrier, count)
            pl.semaphore_signal(ready, inc=1, device_id=sibling, device_id_type=MESH)

        @pl.when(q != core)
        def _():
            pl.semaphore_wait(ready, 1)

    hear(0, 15)

    pm_z = (2 * z + 12 - y) % 8
    pm_slot = ((y + 9 - z) % 8) // 4
    sends_pm = q == x // 2
    hands_on = (y + z) % 2 == 0

    def pm_args(core):
        first = (x % 2) * 256 + (pm_z % 2) * 128 + core * 64
        return (
            jnp.logical_and(pm_z == z, q == core),
            panels_hbm.at[pm_z // 4, pl.ds(pl.multiple_of(first, 64), 64), :], pm.at[pm_slot],
            pm_send.at[core], pm_recv.at[pm_slot], (pm_z * 2 + core, col),
        )

    def pf_args(turn):
        via = ((y + z) // 2 + 2 + 4 * turn) % 8
        slot = ((y + 9 - via) % 8) // 4
        return slot, (via == y, pm.at[slot], pf, pf_send.at[slot], pf_recv, (row, via * 4 + x))

    @pl.when(sends_pm)
    def _():
        for core in range(2):
            start(*pm_args(core))

    load_a.wait()
    high, low = split(a_v[...].T)
    lhs[0:256] = high
    lhs[256:512] = low
    load_pattern.wait()

    @pl.loop(0, 4)
    def _(step):
        p = pair(step)
        load_u(p).wait()
        parts = []
        for b in range(4):
            keep = pattern[p // 2, row * 4 + b].astype(F32)
            parts.append(u_v[p, b * 128:(b + 1) * 128] * jnp.full((128, 256), keep, F32).astype(BF16))
        both = jnp.dot(lhs[...], jnp.concatenate(parts, 0), preferred_element_type=F32)
        product = both[0:256] + both[256:512]
        for half in range(2):
            for which in range(2):
                first = which * 128 + half * 64
                pb[half, 2 * p + which] = product[first:first + 64]

    def exchange(p):
        return remote(
            pb.at[1 - q, pl.ds(2 * p, 2)], xb.at[pl.ds(2 * p, 2)], xs_send.at[p], xs_recv.at[p], sibling
        )

    for step in range(4):
        exchange(pair(step)).start()

    def to_z(d):
        there = (d * 2 + q, col)
        return (
            remote(zs.at[d], zr.at[z], zs_send.at[d], zr_recv.at[z], there),
            remote(zsc.at[d], zrsc.at[z], zc_send.at[d], zc_recv.at[z], there),
        )

    hear(1, 62)

    @pl.when(hands_on)
    def _():
        for turn in range(2):
            slot, args = pf_args(turn)
            arrival(pm.at[slot], pm_recv.at[slot]).wait()
            start(*args)

    @pl.loop(0, 8)
    def _(step):
        p, which = pair(step // 2), step % 2
        d = 2 * p + which

        @pl.when(which == 0)
        def _():
            exchange(p).wait_recv()

        total = pb[q, d] + xb[d]

        @pl.when(d == z)
        def _():
            own[...] = total

        @pl.when(d != z)
        def _():
            top = jnp.maximum(jnp.max(jnp.abs(total), axis=0, keepdims=True), TINY)
            zs[d] = jnp.round(total * (TOP / top)).astype(jnp.int32).astype(I16)
            zsc[d] = top * (1.0 / TOP)
            for copy in to_z(d):
                copy.start()

    arrival(pf, pf_recv).wait()
    flipped = pf[...].T
    tb[:, 0:64] = flipped
    tb[:, 64:128] = flipped

    @pl.loop(0, 7)
    def _(step):
        source = (z + far_first(6 - step, 8)) % 8
        arrival(zr.at[source], zr_recv.at[source]).wait()
        arrival(zrsc.at[source], zc_recv.at[source]).wait()
        own[...] += zr[source].astype(jnp.int32).astype(F32) * zrsc[source]
    mask = pattern[z // 4, 2 * col + z % 2].astype(F32)
    block = own[...] * (-mask)
    ipo[...] = block

    def im_args(kk):
        there_x, there_y, there_q = kk, (x % 2) * 4 + (z % 2) * 2 + q, y % 2
        return (
            jnp.logical_and(there_q == q, jnp.logical_and(there_x == x, there_y == y)),
            ipo.at[pl.ds(pl.multiple_of(kk * 16, 16), 16)], im.at[y // 2 * 2 + x // 2], im_send.at[kk], im_recv,
            (z * 2 + there_q, there_y * 4 + there_x),
        )

    high, low = split(block * mask)
    ub_rhs[0:64] = -high
    ub_rhs[64:128] = -low

    def quarter(step):
        return (y // 2 + jnp.where(step == 0, 2, jnp.where(step == 3, 0, 2 * step - 1))) % 4

    def to_sibling(g):
        some = pl.ds(4 * g, 4)
        return remote(ub.at[1 - q, some], ux.at[some], ux_send.at[g], ux_recv.at[g], sibling)

    def to_col(t):
        there = (row, 2 * t + q)
        return (
            remote(uq.at[t], ur.at[col], us_send.at[t], ur_recv, there),
            remote(usc.at[t], ursc.at[col], uc_send.at[t], uc_recv, there),
        )

    @pl.loop(0, 4, unroll=True)
    def _(step):
        g = quarter(step)
        part = jnp.dot(
            tb[pl.ds(pl.multiple_of(g * 128, 128), 128)], ub_rhs[...], preferred_element_type=F32
        ).reshape(4, 2, 16, 256)
        for half in range(2):
            ub[half, pl.ds(4 * g, 4)] = part[:, half]
        to_sibling(g).start()

    sums_here = col % 2 == q

    @pl.loop(0, 4)
    def _(step):
        g = quarter(step)
        to_sibling(g).wait_recv()
        for one in range(4):
            t = 4 * g + one
            total = ub[q, t] + ux[t]
            top = jnp.maximum(jnp.max(jnp.abs(total), axis=0, keepdims=True), TINY)
            uq[t] = jnp.round(total * (TOP / top)).astype(jnp.int32).astype(I16)
            usc[t] = top * (1.0 / TOP)
        for one in range(4):
            t = 4 * g + one

            @pl.when(2 * t + q != col)
            def _():
                for copy in to_col(t):
                    copy.start()

    @pl.loop(0, 4)
    def _(kk):
        start(*im_args(kk))

    def ip_args(k):
        there = (k // 2 * 2 + q) * 2 + k % 2
        return (
            there == row,
            im.at[k], ip_out.at[z // 4, :, pl.ds(pl.multiple_of((z // 2 % 2) * 256, 256), 256)],
            ip_send.at[k], ip_recv, (there, col),
        )

    forwards_ip = (y % 4) // 2 == z % 2

    def to_row(step):
        there = ((z + far_first(step, 8)) % 8 * 2 + q, col)
        return remote(uf, up_all.at[z], uf_send.at[step], uf_recv, there)

    finish = remote(fin, up_out, fin_send, fin_recv, sibling)

    @pl.when(sums_here)
    def _():
        ur[col] = uq[col // 2]
        ursc[col] = usc[col // 2]
        arrival(ur.at[pl.ds(0, 31)], ur_recv).wait()
        arrival(ursc.at[pl.ds(0, 31)], uc_recv).wait()
        uf[...] = jnp.zeros_like(uf)

        @pl.loop(0, 32)
        def _(k):
            uf[...] += ur[k].astype(jnp.int32).astype(F32) * ursc[k]

        @pl.loop(0, 7)
        def _(step):
            to_row(step).start()
        up_all[z] = uf[...]

    @pl.when(forwards_ip)
    def _():
        arrival(im, im_recv).wait()

        @pl.loop(0, 8)
        def _(step):
            start(*ip_args((z // 2 * 2 + 4 + step) % 8))

    @pl.when(sums_here)
    def _():
        arrival(up_all.at[pl.ds(0, 7)], uf_recv).wait()
        for k in range(4):
            fin[k // 2, :, (k % 2) * 256:(k % 2 + 1) * 256] = up_all[2 * k] + up_all[2 * k + 1]
        finish.start()
        pltpu.make_async_copy(fin, up_out, fin_recv).start()

    @pl.when(sends_pm)
    def _():
        for core in range(2):
            sent(*pm_args(core))

    @pl.when(hands_on)
    def _():
        for turn in range(2):
            sent(*pf_args(turn)[1])

    for p in range(4):
        exchange(p).wait_send()

    @pl.loop(1, 8)
    def _(step):
        for copy in to_z((z + step) % 8):
            copy.wait_send()

    @pl.loop(0, 4)
    def _(kk):
        sent(*im_args(kk))

    for g in range(4):
        to_sibling(g).wait_send()

    @pl.loop(0, 16)
    def _(t):
        @pl.when(2 * t + q != col)
        def _():
            for copy in to_col(t):
                copy.wait_send()

    @pl.when(forwards_ip)
    def _():
        @pl.loop(0, 8)
        def _(k):
            sent(*ip_args(k))

    @pl.when(sums_here)
    def _():
        @pl.loop(0, 7)
        def _(step):
            to_row(step).wait_send()

        finish.wait_send()

    arrival(ip_out, ip_recv).wait()
    arrival(up_out, fin_recv).wait()


def shards(inverse_block, panels, pattern):
    dma = pltpu.SemaphoreType.DMA
    return pl.pallas_call(
        kernel,
        out_shape=(
            jax.ShapeDtypeStruct((2, 16, 512), F32),
            jax.ShapeDtypeStruct((2, 16, 512), F32),
        ),
        in_specs=[pl.BlockSpec(memory_space=pltpu.HBM)] * 3,
        out_specs=(pl.BlockSpec(memory_space=pl.ANY), pl.BlockSpec(memory_space=pl.ANY)),
        scratch_shapes=[
            pltpu.SMEM((2, 64), jnp.int32),
            pltpu.VMEM((512, 256), F32),
            pltpu.VMEM((4, 512, 256), BF16),
            pltpu.VMEM((512, 512), BF16),
            pltpu.VMEM((2, 64, 512), BF16),
            pltpu.VMEM((64, 512), BF16),
            pltpu.VMEM((512, 128), BF16),
            pltpu.VMEM((2, 8, 64, 256), F32),
            pltpu.VMEM((8, 64, 256), F32),
            pltpu.VMEM((8, 64, 256), I16),
            pltpu.VMEM((8, 1, 256), F32),
            pltpu.VMEM((8, 64, 256), I16),
            pltpu.VMEM((8, 1, 256), F32),
            pltpu.VMEM((64, 256), F32),
            pltpu.VMEM((8, 16, 256), F32),
            pltpu.VMEM((128, 256), BF16),
            pltpu.VMEM((2, 16, 16, 256), F32),
            pltpu.VMEM((16, 16, 256), F32),
            pltpu.VMEM((16, 16, 256), I16),
            pltpu.VMEM((16, 1, 256), F32),
            pltpu.VMEM((32, 16, 256), I16),
            pltpu.VMEM((32, 1, 256), F32),
            pltpu.VMEM((16, 256), F32),
            pltpu.VMEM((64, 256), F32),
            pltpu.VMEM((8, 16, 256), F32),
            pltpu.VMEM((2, 16, 512), F32),
            dma((6,)), dma((2,)), dma((2,)), dma((2,)), dma, dma((4,)), dma((4,)), dma((8,)), dma((8,)), dma((8,)),
            dma((8,)), dma((4,)), dma, dma((8,)), dma, dma((4,)), dma((4,)), dma((16,)), dma, dma((16,)), dma, dma((7,)), dma, dma, dma,
            pltpu.SemaphoreType.REGULAR,
        ],
        compiler_params=pltpu.CompilerParams(
            collective_id=0, has_side_effects=True, vmem_limit_bytes=56250000
        ),
        cost_estimate=pl.CostEstimate(flops=2 ** 29, bytes_accessed=2 ** 21, transcendentals=0),
    )(pattern, inverse_block, panels)


def solution(mesh):
    return jax.shard_map(
        shards,
        mesh=mesh,
        in_specs=(P("row", "col"), P(None, "row", None), P()),
        out_specs=(P(None, ("row", "col"), None), P(None, "col", None)),
        check_vma=False,
    )
```

```python
import functools

import jax
import jax.numpy as jnp
from jax import lax
from jax.experimental import pallas as pl
from jax.experimental.pallas import tpu as pltpu
from jax.sharding import PartitionSpec as P

MESH = pl.DeviceIdType.MESH
F32 = jnp.float32
BF16 = jnp.bfloat16
I16 = jnp.int16
NZ, NQ, NX, NY = 8, 2, 4, 8
TOP = 32767.0
TINY = 1e-30


def split(value):
    high = value.astype(BF16)
    return high, (value - high.astype(F32)).astype(BF16)


def kernel(
    pattern_hbm, a_hbm, panels_hbm, both_out,
    pattern, a_v, u_v, lhs, pm, pf, tb, pb, xb, zs, zsc, zr, zrsc, own, im, ub_rhs, ub, ux, uq, usc, ur, ursc, uf, ipo, up_all, fin,
    in_sem, pm_send, pm_recv, pf_send, pf_recv, xs_send, xs_recv, zs_send, zr_recv, zc_send, zc_recv,
    im_send, im_recv, ip_send, ip_recv, ux_send, ux_recv, us_send, ur_recv, uc_send, uc_recv, uf_send, uf_recv, fin_send, fin_recv, ready,
):
    ip_out, up_out = both_out.at[0], both_out.at[1]
    row = lax.axis_index("row")
    col = lax.axis_index("col")
    z, q = row // 2, row % 2
    y, x = col // 4, col % 4
    sibling = (row + 1 - 2 * q, col)

    def remote(src, dst, send, recv, there):
        return pltpu.make_async_remote_copy(
            src_ref=src, dst_ref=dst, send_sem=send, recv_sem=recv, device_id=there, device_id_type=MESH
        )

    def arrival(ref, sem):
        return pltpu.make_async_copy(ref, ref, sem)

    def start(here, src, dst, send, recv, there):
        @pl.when(here)
        def _():
            pltpu.make_async_copy(src, dst, recv).start()

        @pl.when(jnp.logical_not(here))
        def _():
            remote(src, dst, send, recv, there).start()

    def sent(here, src, dst, send, recv, there):
        @pl.when(jnp.logical_not(here))
        def _():
            remote(src, dst, send, recv, there).wait_send()

    def far_first(step, count):
        half = (step + 1) // 2
        return count // 2 + jnp.where(step % 2 == 0, half, -half)

    def pair(step):
        return (z // 2 + jnp.where(step == 0, 2, jnp.where(step == 3, 0, 2 * step - 1))) % 4

    def load_u(p):
        return pltpu.make_async_copy(
            panels_hbm.at[p // 2, :, pl.ds(pl.multiple_of((p % 2) * 256, 256), 256)], u_v.at[p], in_sem.at[1 + p]
        )

    load_pattern = pltpu.make_async_copy(pattern_hbm, pattern, in_sem.at[5])
    load_a = pltpu.make_async_copy(a_hbm, a_v, in_sem.at[0])
    load_a.start()
    load_pattern.start()
    for step in range(4):
        load_u(pair(step)).start()

    barrier = pltpu.get_barrier_semaphore()

    @pl.loop(0, 7)
    def _(step):
        there = ((z + far_first(step, 8)) % 8 * 2, col)
        pl.semaphore_signal(barrier, inc=1, device_id=there, device_id_type=MESH)

    @pl.when(q == 1)
    def _():
        pl.semaphore_signal(barrier, inc=1, device_id=sibling, device_id_type=MESH)

    @pl.loop(0, 31)
    def _(step):
        there = (z * 2 + 1, (col + far_first(step, 32)) % 32)
        pl.semaphore_signal(barrier, inc=1, device_id=there, device_id_type=MESH)

    def hear(core, count):
        @pl.when(q == core)
        def _():
            pl.semaphore_wait(barrier, count)
            pl.semaphore_signal(ready, inc=1, device_id=sibling, device_id_type=MESH)

        @pl.when(q != core)
        def _():
            pl.semaphore_wait(ready, 1)

    hear(0, 15)

    pm_z = (2 * z + 12 - y) % 8
    pm_slot = ((y + 9 - z) % 8) // 4
    sends_pm = q == x // 2
    hands_on = (y + z) % 2 == 0

    def pm_args(core):
        first = (x % 2) * 256 + (pm_z % 2) * 128 + core * 64
        return (
            jnp.logical_and(pm_z == z, q == core),
            panels_hbm.at[pm_z // 4, pl.ds(pl.multiple_of(first, 64), 64), :], pm.at[pm_slot],
            pm_send.at[core], pm_recv.at[pm_slot], (pm_z * 2 + core, col),
        )

    def pf_args(turn):
        via = ((y + z) // 2 + 2 + 4 * turn) % 8
        slot = ((y + 9 - via) % 8) // 4
        return slot, (via == y, pm.at[slot], pf, pf_send.at[slot], pf_recv, (row, via * 4 + x))

    @pl.when(sends_pm)
    def _():
        for core in range(2):
            start(*pm_args(core))

    load_a.wait()
    high, low = split(a_v[...].T)
    lhs[0:256] = high
    lhs[256:512] = low
    load_pattern.wait()

    @pl.loop(0, 4)
    def _(step):
        p = pair(step)
        load_u(p).wait()
        parts = []
        for b in range(4):
            keep = pattern[p // 2, row * 4 + b].astype(F32)
            parts.append(u_v[p, b * 128:(b + 1) * 128] * jnp.full((128, 256), keep, F32).astype(BF16))
        both = jnp.dot(lhs[...], jnp.concatenate(parts, 0), preferred_element_type=F32)
        product = both[0:256] + both[256:512]
        for half in range(2):
            for which in range(2):
                first = which * 128 + half * 64
                pb[half, 2 * p + which] = product[first:first + 64]

    def exchange(p):
        return remote(
            pb.at[1 - q, pl.ds(2 * p, 2)], xb.at[pl.ds(2 * p, 2)], xs_send.at[p], xs_recv.at[p], sibling
        )

    for step in range(4):
        exchange(pair(step)).start()

    def to_z(d):
        there = (d * 2 + q, col)
        return (
            remote(zs.at[d], zr.at[z], zs_send.at[d], zr_recv.at[z], there),
            remote(zsc.at[d], zrsc.at[z], zc_send.at[d], zc_recv.at[z], there),
        )

    hear(1, 62)

    @pl.when(hands_on)
    def _():
        for turn in range(2):
            slot, args = pf_args(turn)
            arrival(pm.at[slot], pm_recv.at[slot]).wait()
            start(*args)

    @pl.loop(0, 8)
    def _(step):
        p, which = pair(step // 2), step % 2
        d = 2 * p + which

        @pl.when(which == 0)
        def _():
            exchange(p).wait_recv()

        total = pb[q, d] + xb[d]

        @pl.when(d == z)
        def _():
            own[...] = total

        @pl.when(d != z)
        def _():
            top = jnp.maximum(jnp.max(jnp.abs(total), axis=0, keepdims=True), TINY)
            zs[d] = jnp.round(total * (TOP / top)).astype(jnp.int32).astype(I16)
            zsc[d] = top * (1.0 / TOP)
            for copy in to_z(d):
                copy.start()

    arrival(pf, pf_recv).wait()
    flipped = pf[...].T
    tb[:, 0:64] = flipped
    tb[:, 64:128] = flipped

    @pl.loop(0, 7)
    def _(step):
        source = (z + far_first(6 - step, 8)) % 8
        arrival(zr.at[source], zr_recv.at[source]).wait()
        arrival(zrsc.at[source], zc_recv.at[source]).wait()
        own[...] += zr[source].astype(jnp.int32).astype(F32) * zrsc[source]
    mask = pattern[z // 4, 2 * col + z % 2].astype(F32)
    block = own[...] * (-mask)
    ipo[...] = block

    def im_args(kk):
        there_x, there_y, there_q = kk, (x % 2) * 4 + (z % 2) * 2 + q, y % 2
        return (
            jnp.logical_and(there_q == q, jnp.logical_and(there_x == x, there_y == y)),
            ipo.at[pl.ds(pl.multiple_of(kk * 16, 16), 16)], im.at[y // 2 * 2 + x // 2], im_send.at[kk], im_recv,
            (z * 2 + there_q, there_y * 4 + there_x),
        )

    high, low = split(block * mask)
    ub_rhs[0:64] = -high
    ub_rhs[64:128] = -low

    def quarter(step):
        return (y // 2 + jnp.where(step == 0, 2, jnp.where(step == 3, 0, 2 * step - 1))) % 4

    def to_sibling(g):
        some = pl.ds(4 * g, 4)
        return remote(ub.at[1 - q, some], ux.at[some], ux_send.at[g], ux_recv.at[g], sibling)

    def to_col(t):
        there = (row, 2 * t + q)
        return (
            remote(uq.at[t], ur.at[col], us_send.at[t], ur_recv, there),
            remote(usc.at[t], ursc.at[col], uc_send.at[t], uc_recv, there),
        )

    @pl.loop(0, 4, unroll=True)
    def _(step):
        g = quarter(step)
        part = jnp.dot(
            tb[pl.ds(pl.multiple_of(g * 128, 128), 128)], ub_rhs[...], preferred_element_type=F32
        ).reshape(4, 2, 16, 256)
        for half in range(2):
            ub[half, pl.ds(4 * g, 4)] = part[:, half]
        to_sibling(g).start()

    sums_here = col % 2 == q

    @pl.loop(0, 4)
    def _(step):
        g = quarter(step)
        to_sibling(g).wait_recv()
        for one in range(4):
            t = 4 * g + one
            total = ub[q, t] + ux[t]
            top = jnp.maximum(jnp.max(jnp.abs(total), axis=0, keepdims=True), TINY)
            uq[t] = jnp.round(total * (TOP / top)).astype(jnp.int32).astype(I16)
            usc[t] = top * (1.0 / TOP)
        for one in range(4):
            t = 4 * g + one

            @pl.when(2 * t + q != col)
            def _():
                for copy in to_col(t):
                    copy.start()

    @pl.loop(0, 4)
    def _(kk):
        start(*im_args(kk))

    def ip_args(k):
        there = (k // 2 * 2 + q) * 2 + k % 2
        return (
            there == row,
            im.at[k], ip_out.at[z // 4, :, pl.ds(pl.multiple_of((z // 2 % 2) * 256, 256), 256)],
            ip_send.at[k], ip_recv, (there, col),
        )

    forwards_ip = (y % 4) // 2 == z % 2

    def to_row(step):
        there = ((z + far_first(step, 8)) % 8 * 2 + q, col)
        return remote(uf, up_all.at[z], uf_send.at[step], uf_recv, there)

    finish = remote(fin, up_out, fin_send, fin_recv, sibling)

    @pl.when(sums_here)
    def _():
        ur[col] = uq[col // 2]
        ursc[col] = usc[col // 2]
        arrival(ur.at[pl.ds(0, 31)], ur_recv).wait()
        arrival(ursc.at[pl.ds(0, 31)], uc_recv).wait()
        uf[...] = jnp.zeros_like(uf)

        @pl.loop(0, 32)
        def _(k):
            uf[...] += ur[k].astype(jnp.int32).astype(F32) * ursc[k]

        @pl.loop(0, 7)
        def _(step):
            to_row(step).start()
        up_all[z] = uf[...]

    @pl.when(forwards_ip)
    def _():
        arrival(im, im_recv).wait()

        @pl.loop(0, 8)
        def _(step):
            start(*ip_args((z // 2 * 2 + 4 + step) % 8))

    @pl.when(sums_here)
    def _():
        arrival(up_all.at[pl.ds(0, 7)], uf_recv).wait()
        for k in range(4):
            fin[k // 2, :, (k % 2) * 256:(k % 2 + 1) * 256] = up_all[2 * k] + up_all[2 * k + 1]
        finish.start()
        pltpu.make_async_copy(fin, up_out, fin_recv).start()

    @pl.when(sends_pm)
    def _():
        for core in range(2):
            sent(*pm_args(core))

    @pl.when(hands_on)
    def _():
        for turn in range(2):
            sent(*pf_args(turn)[1])

    for p in range(4):
        exchange(p).wait_send()

    @pl.loop(1, 8)
    def _(step):
        for copy in to_z((z + step) % 8):
            copy.wait_send()

    @pl.loop(0, 4)
    def _(kk):
        sent(*im_args(kk))

    for g in range(4):
        to_sibling(g).wait_send()

    @pl.loop(0, 16)
    def _(t):
        @pl.when(2 * t + q != col)
        def _():
            for copy in to_col(t):
                copy.wait_send()

    @pl.when(forwards_ip)
    def _():
        @pl.loop(0, 8)
        def _(k):
            sent(*ip_args(k))

    @pl.when(sums_here)
    def _():
        @pl.loop(0, 7)
        def _(step):
            to_row(step).wait_send()

        finish.wait_send()

    arrival(ip_out, ip_recv).wait()
    arrival(up_out, fin_recv).wait()


def shards(inverse_block, panels, pattern):
    dma = pltpu.SemaphoreType.DMA
    both = pl.pallas_call(
        kernel,
        out_shape=jax.ShapeDtypeStruct((2, 2, 16, 512), F32),
        in_specs=[pl.BlockSpec(memory_space=pltpu.HBM)] * 3,
        out_specs=pl.BlockSpec(memory_space=pl.ANY),
        scratch_shapes=[
            pltpu.SMEM((2, 64), jnp.int32),
            pltpu.VMEM((512, 256), F32),
            pltpu.VMEM((4, 512, 256), BF16),
            pltpu.VMEM((512, 512), BF16),
            pltpu.VMEM((2, 64, 512), BF16),
            pltpu.VMEM((64, 512), BF16),
            pltpu.VMEM((512, 128), BF16),
            pltpu.VMEM((2, 8, 64, 256), F32),
            pltpu.VMEM((8, 64, 256), F32),
            pltpu.VMEM((8, 64, 256), I16),
            pltpu.VMEM((8, 1, 256), F32),
            pltpu.VMEM((8, 64, 256), I16),
            pltpu.VMEM((8, 1, 256), F32),
            pltpu.VMEM((64, 256), F32),
            pltpu.VMEM((8, 16, 256), F32),
            pltpu.VMEM((128, 256), BF16),
            pltpu.VMEM((2, 16, 16, 256), F32),
            pltpu.VMEM((16, 16, 256), F32),
            pltpu.VMEM((16, 16, 256), I16),
            pltpu.VMEM((16, 1, 256), F32),
            pltpu.VMEM((32, 16, 256), I16),
            pltpu.VMEM((32, 1, 256), F32),
            pltpu.VMEM((16, 256), F32),
            pltpu.VMEM((64, 256), F32),
            pltpu.VMEM((8, 16, 256), F32),
            pltpu.VMEM((2, 16, 512), F32),
            dma((6,)), dma((2,)), dma((2,)), dma((2,)), dma, dma((4,)), dma((4,)), dma((8,)), dma((8,)), dma((8,)),
            dma((8,)), dma((4,)), dma, dma((8,)), dma, dma((4,)), dma((4,)), dma((16,)), dma, dma((16,)), dma, dma((7,)), dma, dma, dma,
            pltpu.SemaphoreType.REGULAR,
        ],
        compiler_params=pltpu.CompilerParams(
            collective_id=0, has_side_effects=True, vmem_limit_bytes=56250000
        ),
        cost_estimate=pl.CostEstimate(flops=2 ** 29, bytes_accessed=2 ** 21, transcendentals=0),
    )(pattern, inverse_block, panels)
    return both[0], both[1]


def solution(mesh):
    return jax.shard_map(
        shards,
        mesh=mesh,
        in_specs=(P("row", "col"), P(None, "row", None), P()),
        out_specs=(P(None, ("row", "col"), None), P(None, "col", None)),
        check_vma=False,
    )
```

```python
import functools

import jax
import jax.numpy as jnp
from jax import lax
from jax.experimental import pallas as pl
from jax.experimental.pallas import tpu as pltpu
from jax.sharding import PartitionSpec as P

MESH = pl.DeviceIdType.MESH
F32 = jnp.float32
BF16 = jnp.bfloat16
I16 = jnp.int16
NZ, NQ, NX, NY = 8, 2, 4, 8
TOP = 32767.0
TINY = 1e-30


def split(value):
    high = value.astype(BF16)
    return high, (value - high.astype(F32)).astype(BF16)


def kernel(
    pattern_hbm, a_hbm, panels_hbm, both_out,
    pattern, a_v, u_v, lhs, pm, pf, tb, pb, xb, zs, zsc, zr, zrsc, own, im, ub_rhs, ub, ux, uq, usc, ur, ursc, uf, ipo, up_all, fin,
    in_sem, pm_send, pm_recv, pf_send, pf_recv, xs_send, xs_recv, zs_send, zr_recv, zc_send, zc_recv,
    im_send, im_recv, ip_send, ip_recv, ux_send, ux_recv, us_send, ur_recv, uc_send, uc_recv, uf_send, uf_recv, fin_send, fin_recv, ready,
):
    ip_out, up_out = both_out.at[0], both_out.at[1]
    row = lax.axis_index("row")
    col = lax.axis_index("col")
    z, q = row // 2, row % 2
    y, x = col // 4, col % 4
    sibling = (row + 1 - 2 * q, col)

    def remote(src, dst, send, recv, there):
        return pltpu.make_async_remote_copy(
            src_ref=src, dst_ref=dst, send_sem=send, recv_sem=recv, device_id=there, device_id_type=MESH
        )

    def arrival(ref, sem):
        return pltpu.make_async_copy(ref, ref, sem)

    def start(here, src, dst, send, recv, there):
        @pl.when(here)
        def _():
            pltpu.make_async_copy(src, dst, recv).start()

        @pl.when(jnp.logical_not(here))
        def _():
            remote(src, dst, send, recv, there).start()

    def sent(here, src, dst, send, recv, there):
        @pl.when(jnp.logical_not(here))
        def _():
            remote(src, dst, send, recv, there).wait_send()

    def far_first(step, count):
        half = (step + 1) // 2
        return count // 2 + jnp.where(step % 2 == 0, half, -half)

    def pair(step):
        return (z // 2 + jnp.where(step == 0, 2, jnp.where(step == 3, 0, 2 * step - 1))) % 4

    def load_u(p):
        return pltpu.make_async_copy(
            panels_hbm.at[p // 2, :, pl.ds(pl.multiple_of((p % 2) * 256, 256), 256)], u_v.at[p], in_sem.at[1 + p]
        )

    load_pattern = pltpu.make_async_copy(pattern_hbm, pattern, in_sem.at[5])
    load_a = pltpu.make_async_copy(a_hbm, a_v, in_sem.at[0])
    load_a.start()
    load_pattern.start()
    for step in range(4):
        load_u(pair(step)).start()

    barrier = pltpu.get_barrier_semaphore()

    @pl.loop(0, 7)
    def _(step):
        there = ((z + far_first(step, 8)) % 8 * 2, col)
        pl.semaphore_signal(barrier, inc=1, device_id=there, device_id_type=MESH)

    @pl.when(q == 1)
    def _():
        pl.semaphore_signal(barrier, inc=1, device_id=sibling, device_id_type=MESH)

    @pl.loop(0, 31)
    def _(step):
        there = (z * 2 + 1, (col + far_first(step, 32)) % 32)
        pl.semaphore_signal(barrier, inc=1, device_id=there, device_id_type=MESH)

    def hear(core, count):
        @pl.when(q == core)
        def _():
            pl.semaphore_wait(barrier, count)
            pl.semaphore_signal(ready, inc=1, device_id=sibling, device_id_type=MESH)

        @pl.when(q != core)
        def _():
            pl.semaphore_wait(ready, 1)

    load_a.wait()
    high, low = split(a_v[...].T)
    lhs[0:256] = high
    lhs[256:512] = low
    load_pattern.wait()

    hear(0, 15)

    pm_z = (2 * z + 12 - y) % 8
    pm_slot = ((y + 9 - z) % 8) // 4
    sends_pm = q == x // 2
    hands_on = (y + z) % 2 == 0

    def pm_args(core):
        first = (x % 2) * 256 + (pm_z % 2) * 128 + core * 64
        return (
            jnp.logical_and(pm_z == z, q == core),
            panels_hbm.at[pm_z // 4, pl.ds(pl.multiple_of(first, 64), 64), :], pm.at[pm_slot],
            pm_send.at[core], pm_recv.at[pm_slot], (pm_z * 2 + core, col),
        )

    def pf_args(turn):
        via = ((y + z) // 2 + 2 + 4 * turn) % 8
        slot = ((y + 9 - via) % 8) // 4
        return slot, (via == y, pm.at[slot], pf, pf_send.at[slot], pf_recv, (row, via * 4 + x))

    @pl.when(sends_pm)
    def _():
        for core in range(2):
            start(*pm_args(core))

    @pl.loop(0, 4)
    def _(step):
        p = pair(step)
        load_u(p).wait()
        parts = []
        for b in range(4):
            keep = pattern[p // 2, row * 4 + b].astype(F32)
            parts.append(u_v[p, b * 128:(b + 1) * 128] * jnp.full((128, 256), keep, F32).astype(BF16))
        both = jnp.dot(lhs[...], jnp.concatenate(parts, 0), preferred_element_type=F32)
        product = both[0:256] + both[256:512]
        for half in range(2):
            for which in range(2):
                first = which * 128 + half * 64
                pb[half, 2 * p + which] = product[first:first + 64]

    def exchange(p):
        return remote(
            pb.at[1 - q, pl.ds(2 * p, 2)], xb.at[pl.ds(2 * p, 2)], xs_send.at[p], xs_recv.at[p], sibling
        )

    for step in range(4):
        exchange(pair(step)).start()

    def to_z(d):
        there = (d * 2 + q, col)
        return (
            remote(zs.at[d], zr.at[z], zs_send.at[d], zr_recv.at[z], there),
            remote(zsc.at[d], zrsc.at[z], zc_send.at[d], zc_recv.at[z], there),
        )

    hear(1, 62)

    @pl.when(hands_on)
    def _():
        for turn in range(2):
            slot, args = pf_args(turn)
            arrival(pm.at[slot], pm_recv.at[slot]).wait()
            start(*args)

    @pl.loop(0, 8)
    def _(step):
        p, which = pair(step // 2), step % 2
        d = 2 * p + which

        @pl.when(which == 0)
        def _():
            exchange(p).wait_recv()

        total = pb[q, d] + xb[d]

        @pl.when(d == z)
        def _():
            own[...] = total

        @pl.when(d != z)
        def _():
            top = jnp.maximum(jnp.max(jnp.abs(total), axis=0, keepdims=True), TINY)
            zs[d] = jnp.round(total * (TOP / top)).astype(jnp.int32).astype(I16)
            zsc[d] = top * (1.0 / TOP)
            for copy in to_z(d):
                copy.start()

    arrival(pf, pf_recv).wait()
    flipped = pf[...].T
    tb[:, 0:64] = flipped
    tb[:, 64:128] = flipped

    @pl.loop(0, 7)
    def _(step):
        source = (z + far_first(6 - step, 8)) % 8
        arrival(zr.at[source], zr_recv.at[source]).wait()
        arrival(zrsc.at[source], zc_recv.at[source]).wait()
        own[...] += zr[source].astype(jnp.int32).astype(F32) * zrsc[source]
    mask = pattern[z // 4, 2 * col + z % 2].astype(F32)
    block = own[...] * (-mask)
    ipo[...] = block

    def im_args(kk):
        there_x, there_y, there_q = kk, (x % 2) * 4 + (z % 2) * 2 + q, y % 2
        return (
            jnp.logical_and(there_q == q, jnp.logical_and(there_x == x, there_y == y)),
            ipo.at[pl.ds(pl.multiple_of(kk * 16, 16), 16)], im.at[y // 2 * 2 + x // 2], im_send.at[kk], im_recv,
            (z * 2 + there_q, there_y * 4 + there_x),
        )

    high, low = split(block * mask)
    ub_rhs[0:64] = -high
    ub_rhs[64:128] = -low

    def quarter(step):
        return (y // 2 + jnp.where(step == 0, 2, jnp.where(step == 3, 0, 2 * step - 1))) % 4

    def to_sibling(g):
        some = pl.ds(4 * g, 4)
        return remote(ub.at[1 - q, some], ux.at[some], ux_send.at[g], ux_recv.at[g], sibling)

    def to_col(t):
        there = (row, 2 * t + q)
        return (
            remote(uq.at[t], ur.at[col], us_send.at[t], ur_recv, there),
            remote(usc.at[t], ursc.at[col], uc_send.at[t], uc_recv, there),
        )

    @pl.loop(0, 4, unroll=True)
    def _(step):
        g = quarter(step)
        part = jnp.dot(
            tb[pl.ds(pl.multiple_of(g * 128, 128), 128)], ub_rhs[...], preferred_element_type=F32
        ).reshape(4, 2, 16, 256)
        for half in range(2):
            ub[half, pl.ds(4 * g, 4)] = part[:, half]
        to_sibling(g).start()

    sums_here = col % 2 == q

    @pl.loop(0, 4)
    def _(step):
        g = quarter(step)
        to_sibling(g).wait_recv()
        for one in range(4):
            t = 4 * g + one
            total = ub[q, t] + ux[t]
            top = jnp.maximum(jnp.max(jnp.abs(total), axis=0, keepdims=True), TINY)
            uq[t] = jnp.round(total * (TOP / top)).astype(jnp.int32).astype(I16)
            usc[t] = top * (1.0 / TOP)
        for one in range(4):
            t = 4 * g + one

            @pl.when(2 * t + q != col)
            def _():
                for copy in to_col(t):
                    copy.start()

    @pl.loop(0, 4)
    def _(kk):
        start(*im_args(kk))

    def ip_args(k):
        there = (k // 2 * 2 + q) * 2 + k % 2
        return (
            there == row,
            im.at[k], ip_out.at[z // 4, :, pl.ds(pl.multiple_of((z // 2 % 2) * 256, 256), 256)],
            ip_send.at[k], ip_recv, (there, col),
        )

    forwards_ip = (y % 4) // 2 == z % 2

    def to_row(step):
        there = ((z + far_first(step, 8)) % 8 * 2 + q, col)
        return remote(uf, up_all.at[z], uf_send.at[step], uf_recv, there)

    finish = remote(fin, up_out, fin_send, fin_recv, sibling)

    @pl.when(sums_here)
    def _():
        ur[col] = uq[col // 2]
        ursc[col] = usc[col // 2]
        arrival(ur.at[pl.ds(0, 31)], ur_recv).wait()
        arrival(ursc.at[pl.ds(0, 31)], uc_recv).wait()
        def add(k, total):
            return total + ur[k].astype(jnp.int32).astype(F32) * ursc[k]

        uf[...] = lax.fori_loop(0, 32, add, jnp.zeros((16, 256), F32), unroll=8)

        @pl.loop(0, 7)
        def _(step):
            to_row(step).start()
        up_all[z] = uf[...]

    @pl.when(forwards_ip)
    def _():
        arrival(im, im_recv).wait()

        @pl.loop(0, 8)
        def _(step):
            start(*ip_args((z // 2 * 2 + 4 + step) % 8))

    @pl.when(sums_here)
    def _():
        arrival(up_all.at[pl.ds(0, 7)], uf_recv).wait()
        for k in range(4):
            fin[k // 2, :, (k % 2) * 256:(k % 2 + 1) * 256] = up_all[2 * k] + up_all[2 * k + 1]
        finish.start()
        pltpu.make_async_copy(fin, up_out, fin_recv).start()

    @pl.when(sends_pm)
    def _():
        for core in range(2):
            sent(*pm_args(core))

    @pl.when(hands_on)
    def _():
        for turn in range(2):
            sent(*pf_args(turn)[1])

    for p in range(4):
        exchange(p).wait_send()

    @pl.loop(1, 8)
    def _(step):
        for copy in to_z((z + step) % 8):
            copy.wait_send()

    @pl.loop(0, 4)
    def _(kk):
        sent(*im_args(kk))

    for g in range(4):
        to_sibling(g).wait_send()

    @pl.loop(0, 16)
    def _(t):
        @pl.when(2 * t + q != col)
        def _():
            for copy in to_col(t):
                copy.wait_send()

    @pl.when(forwards_ip)
    def _():
        @pl.loop(0, 8)
        def _(k):
            sent(*ip_args(k))

    @pl.when(sums_here)
    def _():
        @pl.loop(0, 7)
        def _(step):
            to_row(step).wait_send()

        finish.wait_send()

    arrival(ip_out, ip_recv).wait()
    arrival(up_out, fin_recv).wait()


def shards(inverse_block, panels, pattern):
    dma = pltpu.SemaphoreType.DMA
    both = pl.pallas_call(
        kernel,
        out_shape=jax.ShapeDtypeStruct((2, 2, 16, 512), F32),
        in_specs=[pl.BlockSpec(memory_space=pltpu.HBM)] * 3,
        out_specs=pl.BlockSpec(memory_space=pl.ANY),
        scratch_shapes=[
            pltpu.SMEM((2, 64), jnp.int32),
            pltpu.VMEM((512, 256), F32),
            pltpu.VMEM((4, 512, 256), BF16),
            pltpu.VMEM((512, 512), BF16),
            pltpu.VMEM((2, 64, 512), BF16),
            pltpu.VMEM((64, 512), BF16),
            pltpu.VMEM((512, 128), BF16),
            pltpu.VMEM((2, 8, 64, 256), F32),
            pltpu.VMEM((8, 64, 256), F32),
            pltpu.VMEM((8, 64, 256), I16),
            pltpu.VMEM((8, 1, 256), F32),
            pltpu.VMEM((8, 64, 256), I16),
            pltpu.VMEM((8, 1, 256), F32),
            pltpu.VMEM((64, 256), F32),
            pltpu.VMEM((8, 16, 256), F32),
            pltpu.VMEM((128, 256), BF16),
            pltpu.VMEM((2, 16, 16, 256), F32),
            pltpu.VMEM((16, 16, 256), F32),
            pltpu.VMEM((16, 16, 256), I16),
            pltpu.VMEM((16, 1, 256), F32),
            pltpu.VMEM((32, 16, 256), I16),
            pltpu.VMEM((32, 1, 256), F32),
            pltpu.VMEM((16, 256), F32),
            pltpu.VMEM((64, 256), F32),
            pltpu.VMEM((8, 16, 256), F32),
            pltpu.VMEM((2, 16, 512), F32),
            dma((6,)), dma((2,)), dma((2,)), dma((2,)), dma, dma((4,)), dma((4,)), dma((8,)), dma((8,)), dma((8,)),
            dma((8,)), dma((4,)), dma, dma((8,)), dma, dma((4,)), dma((4,)), dma((16,)), dma, dma((16,)), dma, dma((7,)), dma, dma, dma,
            pltpu.SemaphoreType.REGULAR,
        ],
        compiler_params=pltpu.CompilerParams(
            collective_id=0, has_side_effects=True, vmem_limit_bytes=56250000
        ),
        cost_estimate=pl.CostEstimate(flops=2 ** 29, bytes_accessed=2 ** 21, transcendentals=0),
    )(pattern, inverse_block, panels)
    return both[0], both[1]


def solution(mesh):
    return jax.shard_map(
        shards,
        mesh=mesh,
        in_specs=(P("row", "col"), P(None, "row", None), P()),
        out_specs=(P(None, ("row", "col"), None), P(None, "col", None)),
        check_vma=False,
    )
```
